128 devices in a mesh: row: 4 (over x_hi, core), col: 32 (over x_lo, z, y).
Axes of the slice: x: 4 (x_hi: 2, x_lo: 2; x = x_hi * 2 + x_lo), y: 4, z: 4, core: 2. Of those that a mesh axis runs over, the one named last changes fastest.
Arguments:
- current: bfloat16 [128, 1024, 256], P('row', 'col'), may hold values from -6 to 6
- history: bfloat16 [4, 128, 1024, 256], P(None, 'row', 'col'), may hold values from -6 to 6
- validity: int32 [4, 128, 1024], P(None, 'row', 'col'), may hold values 0 or 1
- offsets: int32 [4, 2], replicated, may hold values from 2 to 30, as said below
- merge_weight: bfloat16 [3, 3, 1280, 256], replicated, may hold values from -0.0546875 to 0.0546875
- out_weight: bfloat16 [3, 3, 256, 256], replicated, may hold values from -0.125 to 0.125
- cotangent: bfloat16 [128, 1024, 256], P('row', 'col'), may hold values from -0.016479492 to 0.016479492
Outputs:
- merged: bfloat16 [128, 1024, 256], P('row', 'col')
- merge_grad: float32 [3, 3, 1280, 256], replicated
- out_grad: float32 [3, 3, 256, 256], replicated
The draws below stay inside these ranges and needn't reach their ends.
Inputs may be any that keep to these rules, and one draw needn't show every extreme that they name: offsets[k, 0] lies in 2 to 30 and offsets[k, 1] in 2 to 30; both never fall as k rises; offsets[0] = (2, 2) and offsets[3] = (30, 30).
All inputs are finite; a program needn't handle non-finite values. No bound on the sum of `validity` on one device may be relied on, other than what follows from the above.
Results may differ from the reference program's by a relative error of at most 0.0037.
Values may be sent and summed in bfloat16 or wider, within the bound.
No kernel may reach another device: no remote copies, remote signals or barrier semaphores. Data moves between devices by JAX's collectives and lax.ppermute only.
A program may use at most 128 MiB of HBM per device.

```python
import jax
import jax.numpy as jnp
from jax import lax

C = 256
FRAMES = 4
TR = 32
TC = 32
NR = 128
NC = 1024


def draw_offsets(key, part):
    row_moves = jax.random.randint(jax.random.fold_in(key, 11), (FRAMES,), 2, TR - 1)
    col_moves = jax.random.randint(jax.random.fold_in(key, 12), (FRAMES,), 2, TC - 1)
    row_moves = jnp.sort(row_moves).at[0].set(2).at[FRAMES - 1].set(TR - 2)
    col_moves = jnp.sort(col_moves).at[0].set(2).at[FRAMES - 1].set(TC - 2)
    return jnp.stack([row_moves, col_moves], axis=1).astype(jnp.int32)


def touch_ends(drawn, key, smallest, high):
    dims = drawn.shape
    index_at = [jax.random.randint(jax.random.fold_in(key, axis), (), 0, dims[axis]) for axis in range(len(dims))]
    drawn = drawn.at[tuple(index_at)].set(smallest)
    longest = dims.index(max(dims))
    index_at[longest] = (index_at[longest] + 1) % dims[longest]
    return drawn.at[tuple(index_at)].set(high)


def steps_of(key, extent, cuts, least, top_value):
    factor_of, own = 1.0, jax.random.fold_in(key, 6)
    for position, parts in cuts:
        draws = jnp.exp(jax.random.uniform(jax.random.fold_in(own, position), (parts,), jnp.float32, least / len(cuts), top_value / len(cuts)))
        factor_of = factor_of * jnp.repeat(draws, extent[position] // parts).reshape([-1 if axis == position else 1 for axis in range(len(extent))])
    return factor_of


def gaussian(stream_key, shape, scale, reach, cuts=(), kind=jnp.bfloat16):
    result = scale * jax.random.normal(stream_key, shape, jnp.float32)
    if cuts:
        result = result * steps_of(stream_key, shape, cuts, -0.22, 0.18)
    return jnp.clip(result, -reach, reach).astype(kind)


def setup_inputs(seed: int = 0) -> dict:
    key_of = jax.random.split(jax.random.key(seed), 8)
    current = gaussian(key_of[0], (NR, NC, C), 1.0, 6.0, ((0, 4), (1, 32)))
    history = gaussian(key_of[1], (FRAMES, NR, NC, C), 1.0, 6.0, ((1, 4), (2, 32)))
    validity = touch_ends((jax.random.randint(key_of[2], (FRAMES, NR, NC), 0, 4) < 3).astype(jnp.int32), jax.random.fold_in(key_of[2], 1), 0, 1)
    offsets = draw_offsets(jax.random.fold_in(key_of[7], 71), 0)
    merge_weight = gaussian(key_of[4], (3, 3, (FRAMES + 1) * C, C), (9 * (FRAMES + 1) * C) ** -0.5, 0.0546875)
    out_weight = gaussian(key_of[5], (3, 3, C, C), (9 * C) ** -0.5, 0.125)
    cotangent = gaussian(key_of[6], (NR, NC, C), (1.0 / (NR * NC) ** 0.5), 0.016479492, ((0, 4), (1, 32)))
    return dict(current=current, history=history, validity=validity, offsets=offsets, merge_weight=merge_weight, out_weight=out_weight, cotangent=cotangent)


def conv_whole(padded, weight, out_rows, out_cols):
    in_width = padded.shape[-1]
    summed = None
    for row_step in range(3):
        for col_step in range(3):
            window = padded[row_step:row_step + out_rows, col_step:col_step + out_cols].reshape(out_rows * out_cols, in_width)
            partial_sum = jnp.dot(window, weight[row_step, col_step], preferred_element_type=jnp.float32)
            summed = partial_sum if summed is None else summed + partial_sum
    return summed.reshape(out_rows, out_cols, -1)

def weight_grad(padded, back, out_rows, out_cols):
    in_width = padded.shape[-1]
    flat_back = back.reshape(out_rows * out_cols, -1)
    rows_list = []
    for row_step in range(3):
        cols_list = []
        for col_step in range(3):
            window = padded[row_step:row_step + out_rows, col_step:col_step + out_cols].reshape(out_rows * out_cols, in_width)
            cols_list.append(jnp.dot(window.T, flat_back, preferred_element_type=jnp.float32))
        rows_list.append(jnp.stack(cols_list))
    return jnp.stack(rows_list)

def reference(current, history, validity, offsets, merge_weight, out_weight, cotangent):
    grid_rows, grid_cols, width = current.shape
    masked = history * validity.astype(jnp.bfloat16)[..., None]
    pieces = [current]
    for frame in range(FRAMES):
        padded = jnp.pad(masked[frame], ((TR, 0), (TC, 0), (0, 0)))
        start_row = (TR - offsets[frame, 0]).astype(jnp.int32)
        start_col = (TC - offsets[frame, 1]).astype(jnp.int32)
        pieces.append(lax.dynamic_slice(padded, (start_row, start_col, jnp.int32(0)), (grid_rows, grid_cols, width)))
    stacked = jnp.concatenate(pieces, axis=-1)
    stacked_pad = jnp.pad(stacked, ((1, 1), (1, 1), (0, 0)))
    pre = conv_whole(stacked_pad, merge_weight, grid_rows, grid_cols)
    hidden = jax.nn.silu(pre).astype(jnp.bfloat16)
    hidden_pad = jnp.pad(hidden, ((1, 1), (1, 1), (0, 0)))
    merged = (current.astype(jnp.float32) + conv_whole(hidden_pad, out_weight, grid_rows, grid_cols)).astype(jnp.bfloat16)
    out_grad = weight_grad(hidden_pad, cotangent, grid_rows, grid_cols)
    grad_pad = jnp.pad(cotangent, ((1, 1), (1, 1), (0, 0)))
    back_hidden = None
    for row_step in range(3):
        for col_step in range(3):
            window = grad_pad[2 - row_step:2 - row_step + grid_rows, 2 - col_step:2 - col_step + grid_cols].reshape(grid_rows * grid_cols, width)
            partial_sum = jnp.dot(window, out_weight[row_step, col_step].T, preferred_element_type=jnp.float32)
            back_hidden = partial_sum if back_hidden is None else back_hidden + partial_sum
    back_hidden = back_hidden.reshape(grid_rows, grid_cols, width)
    sigma = jax.nn.sigmoid(pre)
    back_pre = (back_hidden * (sigma * (1.0 + pre * (1.0 - sigma)))).astype(jnp.bfloat16)
    merge_grad = weight_grad(stacked_pad, back_pre, grid_rows, grid_cols)
    return (merged, merge_grad, out_grad)
```

```python
import jax
import jax.numpy as jnp
from jax import lax
from jax.sharding import Mesh, PartitionSpec as P


def shifted(x, axis, by):
    peers = lax.axis_size(axis)
    pairs = [(i, i + by) for i in range(peers) if 0 <= i + by < peers]
    return lax.ppermute(x, axis, pairs)


def extended(x, sides, width):
    for axis, dim in sides:
        peers, length = (lax.axis_size(axis), x.shape[dim])
        up = [(i, (i + 1) % peers) for i in range(peers - 1)]
        down = [(j, i) for i, j in up]
        last = lax.slice_in_dim(x, length - width, length, axis=dim)
        initial = lax.slice_in_dim(x, 0, width, axis=dim)
        before = lax.ppermute(last, axis, up)
        after = lax.ppermute(initial, axis, down)
        x = jnp.concatenate([before, x, after], axis=dim)
    return x


def conv_apply(padded, weight, out_rows, out_cols):
    in_width = padded.shape[-1]
    summed = None
    for row_step in range(3):
        for col_step in range(3):
            window = padded[row_step : row_step + out_rows, col_step : col_step + out_cols].reshape(
                out_rows * out_cols, in_width
            )
            partial_sum = jnp.dot(
                window, weight[row_step, col_step], preferred_element_type=jnp.float32
            )
            summed = partial_sum if summed is None else summed + partial_sum
    return summed.reshape(out_rows, out_cols, -1)


def weight_grad(padded, back, out_rows, out_cols):
    in_width = padded.shape[-1]
    flat_back = back.reshape(out_rows * out_cols, -1)
    rows_list = []
    for row_step in range(3):
        cols_list = []
        for col_step in range(3):
            window = padded[row_step : row_step + out_rows, col_step : col_step + out_cols].reshape(
                out_rows * out_cols, in_width
            )
            cols_list.append(
                lax.dot_general(
                    window, flat_back, (((0,), (0,)), ((), ())), preferred_element_type=jnp.float32
                )
            )
        rows_list.append(jnp.stack(cols_list))
    return jnp.stack(rows_list)


CHIPS = ("xh", "xl", "z", "y")
ROW = ("xh", "core")
COL = ("xl", "z", "y")


def summed_over_devices(local_merge, local_out):
    width = local_merge.shape[-1]
    half = width // 2
    flat = jnp.concatenate(
        [local_merge.reshape(-1, width), local_out.reshape(-1, width)], axis=0
    )
    merge_rows = local_merge.size // width
    chips = lax.axis_size(CHIPS)
    first = lax.axis_index("core") == 0
    low, high = flat[:, :half], flat[:, half:]
    send = jnp.where(first, high, low).astype(jnp.bfloat16)
    keep = jnp.where(first, low, high)
    pair = keep + lax.ppermute(send, "core", [(0, 1), (1, 0)]).astype(jnp.float32)
    blocks = pair.astype(jnp.bfloat16).reshape(chips, -1, half)
    got = lax.all_to_all(blocks, CHIPS, split_axis=0, concat_axis=0)
    share = jnp.sum(got.astype(jnp.float32), axis=0).astype(jnp.bfloat16)
    spread = jnp.broadcast_to(share[None], blocks.shape)
    own = lax.all_to_all(spread, CHIPS, split_axis=0, concat_axis=0).reshape(-1, half)
    other = lax.ppermute(own, "core", [(0, 1), (1, 0)])
    low = jnp.where(first, own, other).astype(jnp.float32)
    high = jnp.where(first, other, own).astype(jnp.float32)
    whole = jnp.concatenate([low, high], axis=1)
    return (
        whole[:merge_rows].reshape(local_merge.shape),
        whole[merge_rows:].reshape(local_out.shape),
    )


def shards(current, history, validity, offsets, merge_weight, out_weight, cotangent):
    tile_rows, tile_cols, width = current.shape
    frames = history.shape[0]
    masked = history * validity.astype(jnp.bfloat16)[..., None]
    above = shifted(masked, ROW, 1)
    beside = shifted(masked, COL, 1)
    corner = shifted(beside, ROW, 1)
    joined = jnp.concatenate(
        [jnp.concatenate([corner, above], axis=2), jnp.concatenate([beside, masked], axis=2)],
        axis=1,
    )
    margin = 1
    ext_rows = tile_rows + 2 * margin
    ext_cols = tile_cols + 2 * margin
    row_place = lax.axis_index(ROW) * tile_rows - margin + jnp.arange(ext_rows, dtype=jnp.int32)
    col_place = lax.axis_index(COL) * tile_cols - margin + jnp.arange(ext_cols, dtype=jnp.int32)
    row_inside = (row_place >= 0) & (row_place < tile_rows * lax.axis_size(ROW))
    col_inside = (col_place >= 0) & (col_place < tile_cols * lax.axis_size(COL))
    inside = (row_inside[:, None] & col_inside[None, :]).astype(jnp.bfloat16)[..., None]
    current_pad = extended(current, ((ROW, 0), (COL, 1)), margin)
    pieces = [current_pad]
    for frame in range(frames):
        start_row = tile_rows - margin - offsets[frame, 0]
        start_col = tile_cols - margin - offsets[frame, 1]
        window = lax.dynamic_slice(
            joined[frame], (start_row, start_col, jnp.int32(0)), (ext_rows, ext_cols, width)
        )
        pieces.append(window * inside)
    stacked = jnp.concatenate(pieces, axis=-1)
    pre = conv_apply(stacked, merge_weight, tile_rows, tile_cols)
    hidden = jax.nn.silu(pre).astype(jnp.bfloat16)
    hidden_pad = extended(hidden, ((ROW, 0), (COL, 1)), 1)
    merged = (
        current.astype(jnp.float32) + conv_apply(hidden_pad, out_weight, tile_rows, tile_cols)
    ).astype(jnp.bfloat16)
    grad_pad = extended(cotangent, ((ROW, 0), (COL, 1)), 1)
    local_out = weight_grad(hidden_pad, cotangent, tile_rows, tile_cols)
    back_hidden = None
    for row_step in range(3):
        for col_step in range(3):
            window = grad_pad[
                2 - row_step : 2 - row_step + tile_rows, 2 - col_step : 2 - col_step + tile_cols
            ].reshape(tile_rows * tile_cols, width)
            partial_sum = lax.dot_general(
                window,
                out_weight[row_step, col_step],
                (((1,), (1,)), ((), ())),
                preferred_element_type=jnp.float32,
            )
            back_hidden = partial_sum if back_hidden is None else back_hidden + partial_sum
    back_hidden = back_hidden.reshape(tile_rows, tile_cols, width)
    sigma = jax.nn.sigmoid(pre)
    back_pre = (back_hidden * (sigma * (1.0 + pre * (1.0 - sigma)))).astype(jnp.bfloat16)
    local_merge = weight_grad(stacked, back_pre, tile_rows, tile_cols)
    merge_grad, out_grad = summed_over_devices(local_merge, local_out)
    return (merged, merge_grad, out_grad)


def solution(mesh):
    parts = Mesh(mesh.devices.reshape(2, 2, 2, 4, 4), ("xh", "core", "xl", "z", "y"))
    return jax.shard_map(
        shards,
        mesh=parts,
        in_specs=(
            P(ROW, COL, None),
            P(None, ROW, COL, None),
            P(None, ROW, COL),
            P(),
            P(),
            P(),
            P(ROW, COL, None),
        ),
        out_specs=(P(ROW, COL, None), P(), P()),
        check_vma=False,
    )
```

```python
import jax
import jax.numpy as jnp
from jax import lax
from jax.experimental import pallas as pl
from jax.experimental.pallas import tpu as pltpu
from jax.sharding import Mesh, PartitionSpec as P

CHIPS = ("xh", "xl", "z", "y")
ROW = ("xh", "core")
COL = ("xl", "z", "y")
BF16 = jnp.bfloat16
F32 = jnp.float32
SWAP = [(0, 1), (1, 0)]
PARAMS = pltpu.CompilerParams(
    dimension_semantics=("arbitrary",), vmem_limit_bytes=56 * 1024 * 1024
)
WHOLE = pl.BlockSpec(memory_space=pltpu.VMEM)


def moved(x, axis, by):
    peers = lax.axis_size(axis)
    return lax.ppermute(x, axis, [(i, i + by) for i in range(peers) if 0 <= i + by < peers])


def forward_kernel(start_ref, joined_ref, weight_ref, out_weight_ref, stacked_ref, hidden_ref,
                   back_ref, wide, grads, total, back_total):
    step = pl.program_id(0)
    rows, cols, width = stacked_ref.shape[1], stacked_ref.shape[2], wide.shape[-1]
    tile = rows - 2
    layers = stacked_ref.shape[-1] // width

    def spread(write):
        start = start_ref[step]

        turn = jnp.where(start == 0, 0, 2 * cols - start)

        def widen(i, carry):
            wide[i] = pltpu.roll(joined_ref[0, i].astype(F32), turn, 0)
            return carry

        lax.fori_loop(0, rows, widen, 0)

        def shift(i, carry):
            for col_step in range(3):
                write(i, col_step, wide[i, col_step : col_step + cols, :].astype(BF16))
            return carry

        lax.fori_loop(0, rows, shift, 0)

    @pl.when(step < layers)
    def _():
        place = pl.multiple_of(step * width, width)

        def write(i, col_step, value):
            stacked_ref[col_step, i, :, pl.ds(place, width)] = value

        spread(write)

    @pl.when(step == layers)
    def _():
        def write(i, col_step, value):
            grads[col_step, i] = value

        spread(write)
        total[...] = jnp.zeros_like(total)
        back_total[...] = jnp.zeros_like(back_total)

    @pl.when(step > layers)
    def _():
        tap = step - layers - 1
        row_step, col_step = tap // 3, tap % 3
        window = stacked_ref[col_step, pl.ds(row_step, tile)].reshape(tile * cols, -1)
        total[...] += jnp.dot(window, weight_ref[0], preferred_element_type=F32)
        other = grads[2 - col_step, pl.ds(2 - row_step, tile)].reshape(tile * cols, width)
        back_total[...] += lax.dot_general(
            other, out_weight_ref[0], (((1,), (1,)), ((), ())), preferred_element_type=F32
        )

    @pl.when(step == layers + 9)
    def _():
        pre = total[...]
        sigma = jax.nn.sigmoid(pre)
        hidden_ref[...] = (pre * sigma).astype(BF16)
        back_ref[...] = (back_total[...] * (sigma * (1.0 + pre * (1.0 - sigma)))).astype(BF16)


def forward(starts, joined, merge_weight, out_weight, tile, cols):
    layers, rows, _, width = joined.shape
    frames = layers - 1
    cells = tile * cols
    return pl.pallas_call(
        forward_kernel,
        grid=(layers + 9,),
        in_specs=[
            pl.BlockSpec(memory_space=pltpu.SMEM),
            pl.BlockSpec((1,) + joined.shape[1:], lambda i: (jnp.minimum(i, frames), 0, 0, 0)),
            pl.BlockSpec(
                (1, frames * width, width), lambda i: (jnp.maximum(i - layers, 0), 0, 0)
            ),
            pl.BlockSpec((1, width, width), lambda i: (jnp.maximum(i - layers, 0), 0, 0)),
        ],
        out_specs=[
            pl.BlockSpec((3, rows, cols, frames * width), lambda i: (0, 0, 0, 0)),
            pl.BlockSpec((cells, width), lambda i: (0, 0)),
            pl.BlockSpec((cells, width), lambda i: (0, 0)),
        ],
        out_shape=[
            jax.ShapeDtypeStruct((3, rows, cols, frames * width), BF16),
            jax.ShapeDtypeStruct((cells, width), BF16),
            jax.ShapeDtypeStruct((cells, width), BF16),
        ],
        scratch_shapes=[
            pltpu.VMEM(joined.shape[1:], F32),
            pltpu.VMEM((3, rows, cols, width), BF16),
            pltpu.VMEM((cells, width), F32),
            pltpu.VMEM((cells, width), F32),
        ],
        compiler_params=PARAMS,
        name="forward",
    )(starts, joined, merge_weight, out_weight)


def split_halves(core, value, keep_ref, send_ref):
    half = value.shape[-1] // 2
    low, high = value[:, :half], value[:, half:]
    first = core == 0
    keep_ref[...] = jnp.where(first, low, high)
    send_ref[...] = jnp.where(first, high, low).astype(BF16)


def merge_grad_kernel(core_ref, stacked_ref, back_ref, keep_ref, send_ref):
    row_step = pl.program_id(0) % 3
    tile = stacked_ref.shape[1] - 2
    window = stacked_ref[0, pl.ds(row_step, tile)].reshape(back_ref.shape[0], -1)
    value = lax.dot_general(
        window, back_ref[...], (((0,), (0,)), ((), ())), preferred_element_type=F32
    )
    split_halves(core_ref[0], value, keep_ref, send_ref)


def merge_gradient(core, stacked, back_pre):
    _, rows, cols, depth = stacked.shape
    half = back_pre.shape[-1] // 2

    def place(i):
        return ((i % 3) * 3 + i // 3, 0)

    return pl.pallas_call(
        merge_grad_kernel,
        grid=(9,),
        in_specs=[
            pl.BlockSpec(memory_space=pltpu.SMEM),
            pl.BlockSpec((1, rows, cols, depth), lambda i: (i // 3, 0, 0, 0)),
            pl.BlockSpec(back_pre.shape, lambda i: (0, 0)),
        ],
        out_specs=[pl.BlockSpec((depth, half), place), pl.BlockSpec((depth, half), place)],
        out_shape=[
            jax.ShapeDtypeStruct((9 * depth, half), F32),
            jax.ShapeDtypeStruct((9 * depth, half), BF16),
        ],
        compiler_params=PARAMS,
        name="merge_gradient",
    )(core, stacked, back_pre)


def out_kernel(core_ref, hidden_ref, current_ref, cotangent_ref, weight_ref, merged_ref, keep_ref,
               send_ref, shifted, total):
    step = pl.program_id(0)
    _, rows, cols, width = shifted.shape
    tile = rows - 2

    @pl.when(step == 0)
    def _():
        for col_step in range(3):
            shifted[col_step] = hidden_ref[:, col_step : col_step + cols, :].astype(BF16)
        total[...] = current_ref[...].reshape(tile * cols, width).astype(F32)

    row_step, col_step = step // 3, step % 3
    window = shifted[col_step, pl.ds(row_step, tile)].reshape(tile * cols, width)
    value = lax.dot_general(
        window,
        cotangent_ref[...].reshape(tile * cols, width),
        (((0,), (0,)), ((), ())),
        preferred_element_type=F32,
    )
    split_halves(core_ref[0], value, keep_ref, send_ref)
    total[...] += jnp.dot(window, weight_ref[0], preferred_element_type=F32)

    @pl.when(step == 8)
    def _():
        merged_ref[...] = total[...].astype(BF16).reshape(merged_ref.shape)


def out_step(core, hidden_pad, current, cotangent, out_weight):
    tile, cols, width = current.shape
    half = width // 2
    whole3 = pl.BlockSpec(current.shape, lambda i: (0, 0, 0))
    return pl.pallas_call(
        out_kernel,
        grid=(9,),
        in_specs=[
            pl.BlockSpec(memory_space=pltpu.SMEM),
            pl.BlockSpec(hidden_pad.shape, lambda i: (0, 0, 0)),
            whole3,
            whole3,
            pl.BlockSpec((1, width, width), lambda i: (i, 0, 0)),
        ],
        out_specs=[
            whole3,
            pl.BlockSpec((width, half), lambda i: (i, 0)),
            pl.BlockSpec((width, half), lambda i: (i, 0)),
        ],
        out_shape=[
            jax.ShapeDtypeStruct(current.shape, BF16),
            jax.ShapeDtypeStruct((9 * width, half), F32),
            jax.ShapeDtypeStruct((9 * width, half), BF16),
        ],
        scratch_shapes=[
            pltpu.VMEM((3, tile + 2, cols, width), BF16),
            pltpu.VMEM((tile * cols, width), F32),
        ],
        compiler_params=PARAMS,
        name="out_step",
    )(core, hidden_pad, current, cotangent, out_weight)


def shards(current, history, validity, offsets, merge_weight, out_weight, cotangent):
    tile, cols, width = current.shape
    frames = history.shape[0]
    ext = tile + 2
    core = lax.axis_index("core").astype(jnp.int32).reshape(1)
    valid = validity.astype(BF16)[..., None]
    masked = [history[k] * valid[k] for k in range(frames)]

    above3 = moved(masked[3][1:], ROW, 1)
    above2 = moved(masked[2][1:], ROW, 1)
    packed = moved(
        jnp.concatenate([masked[1][1:], masked[0][-3:], current[-1:], cotangent[-1:]], axis=0), ROW, 1
    )
    below = moved(jnp.concatenate([current[:1], cotangent[:1]], axis=0), ROW, -1)
    above1, above0 = packed[: tile - 1], packed[tile - 1 : tile + 2]
    row_last = lax.axis_index(ROW) == lax.axis_size(ROW) - 1
    col_last = lax.axis_index(COL) == lax.axis_size(COL) - 1
    row_inside = (jnp.arange(ext) < ext - 1) | ~row_last
    row_keep = row_inside.astype(BF16)[:, None, None]

    def rows_of(above, k):
        both = jnp.concatenate([above, masked[k]], axis=0)
        start = (tile - 2 - offsets[k, 0], jnp.int32(0), jnp.int32(0))
        return lax.dynamic_slice(both, start, (ext, cols, width)) * row_keep

    near3 = jnp.concatenate([above3, masked[3][:3]], axis=0) * row_keep
    near2 = rows_of(above2, 2)
    near1 = rows_of(above1, 1)
    near0 = jnp.concatenate([above0, masked[0][: tile - 1]], axis=0) * row_keep
    now = jnp.concatenate([packed[tile + 2 : tile + 3], current, below[:1]], axis=0)
    cot = jnp.concatenate([packed[tile + 3 :], cotangent, below[1:]], axis=0)

    left3 = moved(near3, COL, 1)
    left2 = moved(near2, COL, 1)
    side = moved(
        jnp.concatenate([near1, near0[:, -3:], now[:, -1:], cot[:, -1:]], axis=1), COL, 1
    )
    right = moved(jnp.concatenate([now[:, :1], cot[:, :1]], axis=1), COL, -1)

    blank = jnp.zeros((ext, cols - 2, width), BF16)
    joined = jnp.stack(
        [
            jnp.concatenate([side[:, cols + 3 : cols + 4], now, right[:, :1], blank], axis=1),
            jnp.concatenate([jnp.zeros((ext, cols - 3, width), BF16), side[:, cols : cols + 3], near0], axis=1),
            jnp.concatenate([side[:, :cols], near1], axis=1),
            jnp.concatenate([left2, near2], axis=1),
            jnp.concatenate([left3, near3], axis=1),
            jnp.concatenate([side[:, cols + 4 :], cot, right[:, 1:], blank], axis=1),
        ]
    )
    zero = jnp.zeros((1,), jnp.int32)
    frame_starts = cols - 1 - offsets[:, 1].astype(jnp.int32)
    starts = jnp.concatenate([zero, frame_starts, zero])
    outside = jnp.where(col_last, frame_starts + ext - 1, -1)
    outside = jnp.concatenate([zero - 1, outside, zero - 1])[:, None, None, None]
    place = jnp.arange(2 * cols, dtype=jnp.int32)[None, None, :, None]
    joined = joined * (place != outside).astype(BF16)

    stacked, hidden, back_pre = forward(
        starts,
        joined,
        merge_weight.reshape(9, -1, width),
        out_weight.reshape(9, width, width),
        tile,
        cols,
    )
    hidden = hidden.reshape(tile, cols, width)
    hidden_above = moved(hidden[-1:], ROW, 1)
    hidden_below = moved(hidden[:1], ROW, -1)
    hidden_pad = jnp.concatenate([hidden_above, hidden, hidden_below], axis=0)
    hidden_left = moved(hidden_pad[:, -1:], COL, 1)
    hidden_right = moved(hidden_pad[:, :1], COL, -1)
    hidden_pad = jnp.concatenate([hidden_left, hidden_pad, hidden_right], axis=1).astype(F32)

    merge_keep, merge_send = merge_gradient(core, stacked, back_pre)
    merge_got = lax.ppermute(merge_send, "core", SWAP)
    merged, out_keep, out_send = out_step(
        core, hidden_pad, current, cotangent, out_weight.reshape(9, width, width)
    )
    out_got = lax.ppermute(out_send, "core", SWAP)

    chips = lax.axis_size(CHIPS)
    half = width // 2
    pair = jnp.concatenate(
        [
            (merge_keep + merge_got.astype(F32)).astype(BF16),
            (out_keep + out_got.astype(F32)).astype(BF16),
        ],
        axis=0,
    )
    blocks = pair.reshape(chips, -1, half)
    got = lax.all_to_all(blocks, CHIPS, split_axis=0, concat_axis=0)
    share = jnp.sum(got.astype(F32), axis=0).astype(BF16)
    spread = jnp.broadcast_to(share[None], blocks.shape)
    own = lax.all_to_all(spread, CHIPS, split_axis=0, concat_axis=0).reshape(-1, half)
    other = lax.ppermute(own, "core", SWAP)
    first = core[0] == 0
    merge_rows = merge_keep.shape[0]

    def both(begin, end):
        a, b = own[begin:end], other[begin:end]
        return jnp.concatenate([jnp.where(first, a, b), jnp.where(first, b, a)], axis=1).astype(F32)

    merge_grad = both(0, merge_rows).reshape(merge_weight.shape)
    out_grad = both(merge_rows, own.shape[0]).reshape(out_weight.shape)
    return (merged, merge_grad, out_grad)


def solution(mesh):
    parts = Mesh(mesh.devices.reshape(2, 2, 2, 4, 4), ("xh", "core", "xl", "z", "y"))
    return jax.shard_map(
        shards,
        mesh=parts,
        in_specs=(
            P(ROW, COL, None),
            P(None, ROW, COL, None),
            P(None, ROW, COL),
            P(),
            P(),
            P(),
            P(ROW, COL, None),
        ),
        out_specs=(P(ROW, COL, None), P(), P()),
        check_vma=False,
    )
```

```python
import functools

import jax
import jax.numpy as jnp
from jax import lax
from jax.experimental import pallas as pl
from jax.experimental.pallas import tpu as pltpu
from jax.sharding import Mesh, PartitionSpec as P

CHIPS = ("xh", "xl", "z", "y")
ROW = ("xh", "core")
COL = ("xl", "z", "y")
BF16 = jnp.bfloat16
F32 = jnp.float32
SWAP = [(0, 1), (1, 0)]


def work(products, moved_bytes):
    return pl.CostEstimate(flops=2 * products, transcendentals=0, bytes_accessed=moved_bytes)


PARAMS = pltpu.CompilerParams(
    dimension_semantics=("arbitrary",), vmem_limit_bytes=56 * 1024 * 1024
)
WHOLE = pl.BlockSpec(memory_space=pltpu.VMEM)


def moved(x, axis, by):
    peers = lax.axis_size(axis)
    return lax.ppermute(x, axis, [(i, i + by) for i in range(peers) if 0 <= i + by < peers])


def own_half_first(core, value):
    half = value.shape[-1] // 2
    low, high = value[:, :half], value[:, half:]
    first = core == 0
    return jnp.concatenate([jnp.where(first, low, high), jnp.where(first, high, low)], axis=1)


def forward_kernel(core_ref, joined_ref, weight_ref, out_weight_ref, stacked_ref, hidden_ref,
                   back_ref, even, odd, total, back_total):
    step = pl.program_id(0)
    steps = pl.num_programs(0)
    _, rows, cols, width = even.shape
    tile = rows - 2

    def taps(now, before, shifting, multiply):
        def tap(t, carry):
            if multiply is not None:
                multiply(t, before)
            if shifting:
                for more in range(4):
                    row = jnp.minimum(4 * t + more, rows - 1)
                    value = joined_ref[0, row]
                    wide = value.astype(F32)
                    for col_step in range(3):
                        if col_step == 0:
                            part = value[:cols]
                        else:
                            part = wide[col_step : col_step + cols].astype(BF16)
                        now[col_step, row] = part
                        stacked_ref[0, col_step, row] = part
            return carry

        lax.fori_loop(0, 9, tap, 0, unroll=True)

    def forward_tap(t, before):
        window = before[t % 3, pl.ds(t // 3, tile)].reshape(tile * cols, width)
        total[...] += jnp.dot(window, weight_ref[t], preferred_element_type=F32)

    def back_tap(t, before):
        window = before[2 - t % 3, pl.ds(2 - t // 3, tile)].reshape(tile * cols, width)
        back_total[...] += lax.dot_general(
            window, out_weight_ref[t], (((1,), (1,)), ((), ())), preferred_element_type=F32
        )

    @pl.when(step == 0)
    def _():
        total[...] = jnp.zeros_like(total)
        back_total[...] = jnp.zeros_like(back_total)
        taps(even, odd, True, None)

    @pl.when(step == 1)
    def _():
        taps(odd, even, True, back_tap)

    @pl.when((step > 1) & (step < steps - 1) & (step % 2 == 0))
    def _():
        taps(even, odd, True, forward_tap)

    @pl.when((step > 1) & (step < steps - 1) & (step % 2 == 1))
    def _():
        taps(odd, even, True, forward_tap)

    @pl.when(step == steps - 1)
    def _():
        taps(even, odd, False, forward_tap)
        pre = total[...]
        sigma = jax.nn.sigmoid(pre)
        hidden_ref[...] = (pre * sigma).astype(BF16)
        back = back_total[...] * (sigma * (1.0 + pre * (1.0 - sigma)))
        back_ref[...] = own_half_first(core_ref[0], back).astype(BF16)


def forward(core, joined, merge_weight, out_weight):
    layers, rows, wide_cols, width = joined.shape
    cols = wide_cols - 2
    frames = layers - 1
    cells = (rows - 2) * cols
    return pl.pallas_call(
        forward_kernel,
        grid=(layers + 1,),
        in_specs=[
            pl.BlockSpec(memory_space=pltpu.SMEM),
            pl.BlockSpec((1,) + joined.shape[1:], lambda i: (jnp.minimum(i, frames), 0, 0, 0)),
            pl.BlockSpec((9, width, width), lambda i: (0, jnp.maximum(i - 2, 0), 0)),
            pl.BlockSpec((9, width, width), lambda i: (0, 0, 0)),
        ],
        out_specs=[
            pl.BlockSpec(
                (1, 3, rows, cols, width),
                lambda i: (jnp.clip(i - 1, 0, frames - 1), 0, 0, 0, 0),
            ),
            pl.BlockSpec((cells, width), lambda i: (0, 0)),
            pl.BlockSpec((cells, width), lambda i: (0, 0)),
        ],
        out_shape=[
            jax.ShapeDtypeStruct((frames, 3, rows, cols, width), BF16),
            jax.ShapeDtypeStruct((cells, width), BF16),
            jax.ShapeDtypeStruct((cells, width), BF16),
        ],
        scratch_shapes=[
            pltpu.VMEM((3, rows, cols, width), BF16),
            pltpu.VMEM((3, rows, cols, width), BF16),
            pltpu.VMEM((cells, width), F32),
            pltpu.VMEM((cells, width), F32),
        ],
        compiler_params=PARAMS,
        cost_estimate=work(9 * cells * width * width * layers, 25_000_000),
        name="forward",
    )(core, joined, merge_weight, out_weight)


def merge_grad_kernel(stacked_ref, back_ref, *refs):
    keep_ref, send_ref = refs[-2:]
    row_step = pl.program_id(0) % 3
    frames, _, rows, _, width = stacked_ref.shape
    half = keep_ref.shape[-1]
    for frame in range(frames):
        window = stacked_ref[frame, 0, pl.ds(row_step, rows - 2)].reshape(-1, width)
        value = lax.dot_general(
            window, back_ref[...], (((0,), (0,)), ((), ())), preferred_element_type=F32
        )
        keep_ref[frame * width : (frame + 1) * width] = value[:, :half]
        send_ref[frame * width : (frame + 1) * width] = value[:, half:].astype(BF16)


def merge_gradient(stacked, back_pre, begin, end, into=()):
    frames, _, rows, cols, width = stacked.shape
    depth = frames * width
    half = width // 2

    def place(i):
        return ((i % 3) * 3 + begin + i // 3, 0)

    return pl.pallas_call(
        merge_grad_kernel,
        grid=(3 * (end - begin),),
        in_specs=[
            pl.BlockSpec(
                (frames, 1, rows, cols, width), lambda i: (0, begin + i // 3, 0, 0, 0)
            ),
            pl.BlockSpec(back_pre.shape, lambda i: (0, 0)),
        ]
        + [pl.BlockSpec(memory_space=pl.ANY)] * len(into),
        out_specs=[pl.BlockSpec((depth, half), place), pl.BlockSpec((depth, half), place)],
        out_shape=[
            jax.ShapeDtypeStruct((9 * depth, half), F32),
            jax.ShapeDtypeStruct((9 * depth, half), BF16),
        ],
        input_output_aliases={2 + k: k for k in range(len(into))},
        compiler_params=PARAMS,
        cost_estimate=work(
            3 * (end - begin) * back_pre.shape[0] * depth * back_pre.shape[1],
            8_000_000 * (end - begin),
        ),
        name="merge_gradient",
    )(stacked, back_pre, *into)


def out_kernel(core_ref, hidden_ref, current_ref, cotangent_ref, weight_ref, merged_ref, keep_ref,
               send_ref, shifted, turned, total):
    row_step = pl.program_id(0)
    _, rows, cols, width = shifted.shape
    tile = rows - 2
    half = width // 2

    @pl.when(row_step == 0)
    def _():
        for col_step in range(3):
            shifted[col_step] = hidden_ref[:, col_step : col_step + cols, :].astype(BF16)
        total[...] = current_ref[...].reshape(tile * cols, width).astype(F32)
        turned[...] = own_half_first(core_ref[0], cotangent_ref[...].reshape(tile * cols, width))

    summed = total[...]
    for col_step in range(3):
        window = shifted[col_step, pl.ds(row_step, tile)].reshape(tile * cols, width)
        value = lax.dot_general(
            window, turned[...], (((0,), (0,)), ((), ())), preferred_element_type=F32
        )
        keep_ref[col_step * width : (col_step + 1) * width] = value[:, :half]
        send_ref[col_step * width : (col_step + 1) * width] = value[:, half:].astype(BF16)
        summed = summed + jnp.dot(window, weight_ref[col_step], preferred_element_type=F32)
    total[...] = summed

    @pl.when(row_step == 2)
    def _():
        merged_ref[...] = total[...].astype(BF16).reshape(merged_ref.shape)


def out_step(core, hidden_pad, current, cotangent, out_weight):
    tile, cols, width = current.shape
    half = width // 2
    whole3 = pl.BlockSpec(current.shape, lambda i: (0, 0, 0))
    return pl.pallas_call(
        out_kernel,
        grid=(3,),
        in_specs=[
            pl.BlockSpec(memory_space=pltpu.SMEM),
            pl.BlockSpec(hidden_pad.shape, lambda i: (0, 0, 0)),
            whole3,
            whole3,
            pl.BlockSpec((3, width, width), lambda i: (i, 0, 0)),
        ],
        out_specs=[
            whole3,
            pl.BlockSpec((3 * width, half), lambda i: (i, 0)),
            pl.BlockSpec((3 * width, half), lambda i: (i, 0)),
        ],
        out_shape=[
            jax.ShapeDtypeStruct(current.shape, BF16),
            jax.ShapeDtypeStruct((9 * width, half), F32),
            jax.ShapeDtypeStruct((9 * width, half), BF16),
        ],
        scratch_shapes=[
            pltpu.VMEM((3, tile + 2, cols, width), BF16),
            pltpu.VMEM((tile * cols, width), BF16),
            pltpu.VMEM((tile * cols, width), F32),
        ],
        compiler_params=PARAMS,
        cost_estimate=work(18 * tile * cols * width * width, 8_000_000),
        name="out_step",
    )(core, hidden_pad, current, cotangent, out_weight)


def pair_kernel(many, keep_a, got_a, keep_b, got_b, pair_ref):
    step = pl.program_id(0)

    @pl.when(step < many)
    def _():
        pair_ref[...] = (keep_a[...] + got_a[...].astype(F32)).astype(BF16)

    @pl.when(step >= many)
    def _():
        pair_ref[...] = (keep_b[...] + got_b[...].astype(F32)).astype(BF16)


BLOCK = 2304


def pair_sums(keep_a, got_a, keep_b, got_b):
    half = keep_a.shape[1]
    many, more = keep_a.shape[0] // BLOCK, keep_b.shape[0] // BLOCK
    at_a = pl.BlockSpec((BLOCK, half), lambda i: (jnp.minimum(i, many - 1), 0))
    at_b = pl.BlockSpec((BLOCK, half), lambda i: (jnp.maximum(i - many, 0), 0))
    return pl.pallas_call(
        functools.partial(pair_kernel, many),
        grid=(many + more,),
        in_specs=[at_a, at_a, at_b, at_b],
        out_specs=pl.BlockSpec((BLOCK, half), lambda i: (i, 0)),
        out_shape=jax.ShapeDtypeStruct(((many + more) * BLOCK, half), BF16),
        compiler_params=PARAMS,
        name="pair_sums",
    )(keep_a, got_a, keep_b, got_b)


def shards(current, history, validity, offsets, merge_weight, out_weight, cotangent):
    tile, cols, width = current.shape
    frames = history.shape[0]
    ext = tile + 2
    core = lax.axis_index("core").astype(jnp.int32).reshape(1)
    valid = validity.astype(BF16)[..., None]
    masked = [history[k] * valid[k] for k in range(frames)]

    row_last = lax.axis_index(ROW) == lax.axis_size(ROW) - 1
    col_last = lax.axis_index(COL) == lax.axis_size(COL) - 1
    row_inside = (jnp.arange(ext) < ext - 1) | ~row_last
    ext_cols = cols + 2
    col_inside = (jnp.arange(ext_cols) < ext_cols - 1) | ~col_last
    inside = (row_inside[:, None] & col_inside[None, :]).astype(BF16)[..., None]

    own12 = jnp.concatenate([masked[1], masked[2]], axis=0)
    left12 = moved(own12, COL, 1)
    packed = moved(
        jnp.concatenate([masked[3][1:], masked[0][-3:], current[-1:], cotangent[-1:]], axis=0), ROW, 1
    )
    below = moved(jnp.concatenate([current[:1], cotangent[:1]], axis=0), ROW, -1)
    above3, above0 = packed[: tile - 1], packed[tile - 1 : tile + 2]
    near3 = jnp.concatenate([above3, masked[3][:3]], axis=0)
    near0 = jnp.concatenate([above0, masked[0][: tile - 1]], axis=0)
    now = jnp.concatenate([packed[tile + 2 : tile + 3], current, below[:1]], axis=0)
    cot = jnp.concatenate([packed[tile + 3 :], cotangent, below[1:]], axis=0)
    side = moved(
        jnp.concatenate([near3, near0[:, -3:], now[:, -1:], cot[:, -1:]], axis=1), COL, 1
    )
    right = moved(jnp.concatenate([now[:, :1], cot[:, :1]], axis=1), COL, -1)

    left12, right = lax.optimization_barrier((left12, right))

    def cols_of(k):
        part = slice((k - 1) * tile, k * tile)
        wide = jnp.concatenate([left12[part], masked[k]], axis=1)
        start = cols - 1 - offsets[k, 1]
        return lax.dynamic_slice(wide, (jnp.int32(0), start, jnp.int32(0)), (tile, ext_cols, width))

    wide1, wide2 = cols_of(1), cols_of(2)
    above12 = moved(jnp.concatenate([wide1[1:], wide2[1:]], axis=0), ROW, 1)

    def rows_of(above, wide, k):
        both = jnp.concatenate([above, wide], axis=0)
        start = tile - 2 - offsets[k, 0]
        return lax.dynamic_slice(both, (start, jnp.int32(0), jnp.int32(0)), (ext, ext_cols, width)) * inside

    joined = jnp.stack(
        [
            jnp.concatenate([side[:, cols + 4 :], cot, right[:, 1:]], axis=1),
            jnp.concatenate([side[:, cols + 3 : cols + 4], now, right[:, :1]], axis=1),
            jnp.concatenate([side[:, cols : cols + 3], near0[:, : cols - 1]], axis=1) * inside,
            rows_of(above12[: tile - 1], wide1, 1),
            rows_of(above12[tile - 1 :], wide2, 2),
            jnp.concatenate([side[:, 1:cols], near3[:, :3]], axis=1) * inside,
        ]
    )
    stacked, hidden, back_pre = forward(
        core, joined, merge_weight.reshape(9, -1, width), out_weight.reshape(9, width, width)
    )
    hidden = hidden.reshape(tile, cols, width)
    hidden_above = moved(hidden[-1:], ROW, 1)
    hidden_below = moved(hidden[:1], ROW, -1)
    first_taps = merge_gradient(stacked, back_pre, 0, 1)
    back_pre, hidden_above, hidden_below = lax.optimization_barrier(
        (back_pre, hidden_above, hidden_below)
    )
    hidden_pad = jnp.concatenate([hidden_above, hidden, hidden_below], axis=0)
    hidden_left = moved(hidden_pad[:, -1:], COL, 1)
    hidden_right = moved(hidden_pad[:, :1], COL, -1)
    more_taps = merge_gradient(stacked, back_pre, 1, 2, first_taps)
    back_pre, hidden_left, hidden_right = lax.optimization_barrier(
        (back_pre, hidden_left, hidden_right)
    )
    hidden_pad = jnp.concatenate([hidden_left, hidden_pad, hidden_right], axis=1).astype(F32)

    merge_keep, merge_send = merge_gradient(stacked, back_pre, 2, 3, more_taps)
    merge_got = lax.ppermute(merge_send, "core", SWAP)
    merged, out_keep, out_send = out_step(
        core, hidden_pad, current, cotangent, out_weight.reshape(9, width, width)
    )
    out_got = lax.ppermute(out_send, "core", SWAP)

    chips = lax.axis_size(CHIPS)
    half = width // 2
    pair = pair_sums(merge_keep, merge_got, out_keep, out_got)
    blocks = pair.reshape(chips, -1, half)
    got = lax.all_to_all(blocks, CHIPS, split_axis=0, concat_axis=0)
    share = jnp.sum(got.astype(F32), axis=0).astype(BF16)
    spread = jnp.broadcast_to(share[None], blocks.shape)
    own = lax.all_to_all(spread, CHIPS, split_axis=0, concat_axis=0).reshape(-1, half)
    other = lax.ppermute(own, "core", SWAP)
    first = core[0] == 0
    merge_rows = merge_keep.shape[0]

    def both(begin, end):
        a, b = own[begin:end], other[begin:end]
        return jnp.concatenate([jnp.where(first, a, b), jnp.where(first, b, a)], axis=1).astype(F32)

    merge_grad = both(0, merge_rows).reshape(merge_weight.shape)
    out_grad = both(merge_rows, own.shape[0]).reshape(out_weight.shape)
    return (merged, merge_grad, out_grad)


def solution(mesh):
    parts = Mesh(mesh.devices.reshape(2, 2, 2, 4, 4), ("xh", "core", "xl", "z", "y"))
    return jax.shard_map(
        shards,
        mesh=parts,
        in_specs=(
            P(ROW, COL, None),
            P(None, ROW, COL, None),
            P(None, ROW, COL),
            P(),
            P(),
            P(),
            P(ROW, COL, None),
        ),
        out_specs=(P(ROW, COL, None), P(), P()),
        check_vma=False,
    )
```

```python
import functools

import jax
import jax.numpy as jnp
from jax import lax
from jax.experimental import pallas as pl
from jax.experimental.pallas import tpu as pltpu
from jax.sharding import Mesh, PartitionSpec as P

CHIPS = ("xh", "xl", "z", "y")
ROW = ("xh", "core")
COL = ("xl", "z", "y")
BF16 = jnp.bfloat16
F32 = jnp.float32
SWAP = [(0, 1), (1, 0)]


def work(products, moved_bytes):
    return pl.CostEstimate(flops=2 * products, transcendentals=0, bytes_accessed=moved_bytes)


PARAMS = pltpu.CompilerParams(
    dimension_semantics=("arbitrary",), vmem_limit_bytes=56 * 1024 * 1024
)
WHOLE = pl.BlockSpec(memory_space=pltpu.VMEM)


def moved(x, axis, by):
    peers = lax.axis_size(axis)
    return lax.ppermute(x, axis, [(i, i + by) for i in range(peers) if 0 <= i + by < peers])


def shift_row(source, at, target):
    cols = target.shape[2]
    value = source[at]
    wide = value.astype(F32)
    target[0, at[-1]] = value[:cols]
    for col_step in (1, 2):
        target[col_step, at[-1]] = wide[col_step : col_step + cols].astype(BF16)


def forward_kernel(joined_ref, weight_ref, out_weight_ref, hidden_ref, back_ref, even, odd, total,
                   back_total):
    step = pl.program_id(0)
    steps = pl.num_programs(0)
    _, rows, cols, width = even.shape
    tile = rows - 2

    def taps(now, before, shifting, multiply):
        def tap(t, carry):
            if multiply is not None:
                multiply(t, before)
            if shifting:
                for more in range(4):
                    shift_row(joined_ref, (0, jnp.minimum(4 * t + more, rows - 1)), now)
            return carry

        lax.fori_loop(0, 9, tap, 0, unroll=True)

    def forward_tap(t, before):
        window = before[t % 3, pl.ds(t // 3, tile)].reshape(tile * cols, width)
        total[...] += jnp.dot(window, weight_ref[t], preferred_element_type=F32)

    def back_tap(t, before):
        window = before[2 - t % 3, pl.ds(2 - t // 3, tile)].reshape(tile * cols, width)
        back_total[...] += lax.dot_general(
            window, out_weight_ref[t], (((1,), (1,)), ((), ())), preferred_element_type=F32
        )

    @pl.when(step == 0)
    def _():
        total[...] = jnp.zeros_like(total)
        back_total[...] = jnp.zeros_like(back_total)
        taps(even, odd, True, None)

    @pl.when(step == 1)
    def _():
        taps(odd, even, True, back_tap)

    @pl.when((step > 1) & (step < steps - 1) & (step % 2 == 0))
    def _():
        taps(even, odd, True, forward_tap)

    @pl.when((step > 1) & (step < steps - 1) & (step % 2 == 1))
    def _():
        taps(odd, even, True, forward_tap)

    @pl.when(step == steps - 1)
    def _():
        taps(even, odd, False, forward_tap)
        pre = total[...]
        sigma = jax.nn.sigmoid(pre)
        hidden_ref[...] = (pre * sigma).astype(BF16)
        back = back_total[...] * (sigma * (1.0 + pre * (1.0 - sigma)))
        back_ref[...] = back.astype(BF16)


def forward(joined, merge_weight, out_weight):
    layers, rows, wide_cols, width = joined.shape
    cols = wide_cols - 2
    frames = layers - 1
    cells = (rows - 2) * cols
    return pl.pallas_call(
        forward_kernel,
        grid=(layers + 1,),
        in_specs=[
            pl.BlockSpec((1,) + joined.shape[1:], lambda i: (jnp.minimum(i, frames), 0, 0, 0)),
            pl.BlockSpec((9, width, width), lambda i: (0, jnp.maximum(i - 2, 0), 0)),
            pl.BlockSpec((9, width, width), lambda i: (0, 0, 0)),
        ],
        out_specs=[
            pl.BlockSpec((cells, width), lambda i: (0, 0)),
            pl.BlockSpec((cells, width), lambda i: (0, 0)),
        ],
        out_shape=[
            jax.ShapeDtypeStruct((cells, width), BF16),
            jax.ShapeDtypeStruct((cells, width), BF16),
        ],
        scratch_shapes=[
            pltpu.VMEM((3, rows, cols, width), BF16),
            pltpu.VMEM((3, rows, cols, width), BF16),
            pltpu.VMEM((cells, width), F32),
            pltpu.VMEM((cells, width), F32),
        ],
        compiler_params=PARAMS,
        cost_estimate=work(9 * cells * width * width * layers, 25_000_000),
        name="forward",
    )(joined, merge_weight, out_weight)


def layer_kernel(at_ref, own_ref, other_ref, own_right, other_right, *refs):
    out_ref, own_copies, other_copies, held = refs[-4:]
    _, rows, cols, width = own_copies.shape
    tile, half = rows - 2, width // 2

    def product(copies, tap, right):
        window = copies[tap % 3, tap // 3 : tap // 3 + tile].reshape(tile * cols, width)
        return lax.dot_general(
            window, right[...], (((0,), (0,)), ((), ())), preferred_element_type=F32
        )

    for row in range(rows):
        shift_row(own_ref, (0, row), own_copies)
    for tap in range(9):
        held[tap] = product(own_copies, tap, own_right)
        for row in range(4 * tap, min(4 * tap + 4, rows)):
            shift_row(other_ref, (0, row), other_copies)
    for tap in range(9):
        value = held[tap] + product(other_copies, tap, other_right)
        for side in range(2):
            part = value[:, side * half : (side + 1) * half]
            out_ref[0, side, tap * width : (tap + 1) * width] = part.astype(BF16)


def layer_gradient(place, at, own, other, own_right, other_right, into=()):
    _, rows, wide_cols, width = own.shape
    cols = wide_cols - 2
    shape = (3, 2, 9 * width, width // 2)
    window = (1,) + own.shape[1:]
    right = pl.BlockSpec(own_right.shape, lambda i, at: (0, 0))
    return pl.pallas_call(
        layer_kernel,
        grid_spec=pltpu.PrefetchScalarGridSpec(
            num_scalar_prefetch=1,
            grid=(1,),
            in_specs=[
                pl.BlockSpec(window, lambda i, at: (at[0], 0, 0, 0)),
                pl.BlockSpec(window, lambda i, at: (at[1], 0, 0, 0)),
                right,
                right,
            ]
            + [pl.BlockSpec(memory_space=pl.ANY)] * len(into),
            out_specs=pl.BlockSpec((1,) + shape[1:], lambda i, at: (place, 0, 0, 0)),
            scratch_shapes=[
                pltpu.VMEM((3, rows, cols, width), BF16),
                pltpu.VMEM((3, rows, cols, width), BF16),
                pltpu.VMEM((9, width, width), F32),
            ],
        ),
        out_shape=jax.ShapeDtypeStruct(shape, BF16),
        input_output_aliases={5: 0} if into else {},
        compiler_params=PARAMS,
        cost_estimate=work(18 * own_right.shape[0] * width * width, 5_000_000),
        name="layer_gradient",
    )(at, own, other, own_right, other_right, *into)


def merged_kernel(hidden_ref, current_ref, weight_ref, merged_ref, copies, total):
    _, rows, cols, width = copies.shape
    tile = rows - 2
    for row in range(rows):
        shift_row(hidden_ref, (row,), copies)
    total[...] = current_ref[...].reshape(tile * cols, width).astype(F32)
    for tap in range(9):
        window = copies[tap % 3, tap // 3 : tap // 3 + tile].reshape(tile * cols, width)
        total[...] += jnp.dot(window, weight_ref[tap], preferred_element_type=F32)
    merged_ref[...] = total[...].astype(BF16).reshape(merged_ref.shape)


def merged_step(hidden_pad, current, out_weight):
    tile, cols, width = current.shape
    whole = [pl.BlockSpec(x.shape, lambda i: (0, 0, 0)) for x in (hidden_pad, current, out_weight)]
    return pl.pallas_call(
        merged_kernel,
        grid=(1,),
        in_specs=whole,
        out_specs=whole[1],
        out_shape=jax.ShapeDtypeStruct(current.shape, BF16),
        scratch_shapes=[
            pltpu.VMEM((3, tile + 2, cols, width), BF16),
            pltpu.VMEM((tile * cols, width), F32),
        ],
        compiler_params=PARAMS,
        cost_estimate=work(9 * tile * cols * width * width, 4_000_000),
        name="merged_step",
    )(hidden_pad, current, out_weight)


def final_kernel(base_ref, sums_ref, *refs):
    out_ref = refs[-1]
    taps, width, _ = out_ref.shape
    half = sums_ref.shape[-1]

    @pl.when(base_ref[0] + pl.program_id(0) < 5)
    def _():
        for side in range(2):
            part = sums_ref[0, side].reshape(taps, width, half)
            out_ref[:, :, side * half : (side + 1) * half] = part.astype(F32)


def final(base, sums, into=()):
    width = 2 * sums.shape[-1]
    return pl.pallas_call(
        final_kernel,
        grid_spec=pltpu.PrefetchScalarGridSpec(
            num_scalar_prefetch=1,
            grid=(3,),
            in_specs=[pl.BlockSpec((1,) + sums.shape[1:], lambda i, at: (i, 0, 0, 0))]
            + [pl.BlockSpec(memory_space=pl.ANY)] * len(into),
            out_specs=pl.BlockSpec(
                (9, width, width), lambda i, at: (0, jnp.minimum(at[0] + i, 4), 0)
            ),
        ),
        out_shape=jax.ShapeDtypeStruct((9, 5 * width, width), F32),
        input_output_aliases={2: 0} if into else {},
        compiler_params=PARAMS,
        cost_estimate=work(0, 12_000_000),
        name="final",
    )(base, sums, *into)


def shards(current, history, validity, offsets, merge_weight, out_weight, cotangent):
    tile, cols, width = current.shape
    frames = history.shape[0]
    ext = tile + 2
    core = lax.axis_index("core").astype(jnp.int32).reshape(1)
    valid = validity.astype(BF16)[..., None]
    masked12 = history[1:3] * valid[1:3]
    masked12, valid = lax.optimization_barrier((masked12, valid))
    masked = [history[0] * valid[0], masked12[0], masked12[1], history[3] * valid[3]]

    row_last = lax.axis_index(ROW) == lax.axis_size(ROW) - 1
    col_last = lax.axis_index(COL) == lax.axis_size(COL) - 1
    row_inside = (jnp.arange(ext) < ext - 1) | ~row_last
    ext_cols = cols + 2
    col_inside = (jnp.arange(ext_cols) < ext_cols - 1) | ~col_last
    inside = (row_inside[:, None] & col_inside[None, :]).astype(BF16)[..., None]

    left12 = moved(masked12, COL, 1)
    packed = moved(
        jnp.concatenate([masked[3][1:], masked[0][-3:], current[-1:], cotangent[-1:]], axis=0), ROW, 1
    )
    below = moved(jnp.concatenate([current[:1], cotangent[:1]], axis=0), ROW, -1)
    above3, above0 = packed[: tile - 1], packed[tile - 1 : tile + 2]
    near3 = jnp.concatenate([above3, masked[3][:3]], axis=0)
    near0 = jnp.concatenate([above0, masked[0][: tile - 1]], axis=0)
    now = jnp.concatenate([packed[tile + 2 : tile + 3], current, below[:1]], axis=0)
    cot = jnp.concatenate([packed[tile + 3 :], cotangent, below[1:]], axis=0)
    side = moved(
        jnp.concatenate([near3, near0[:, -3:], now[:, -1:], cot[:, -1:]], axis=1), COL, 1
    )
    right = moved(jnp.concatenate([now[:, :1], cot[:, :1]], axis=1), COL, -1)

    left12, right = lax.optimization_barrier((left12, right))

    def cols_of(k):
        wide = jnp.concatenate([left12[k - 1], masked[k]], axis=1)
        start = cols - 1 - offsets[k, 1]
        return lax.dynamic_slice(wide, (jnp.int32(0), start, jnp.int32(0)), (tile, ext_cols, width))

    wide1, wide2 = cols_of(1), cols_of(2)
    above12 = moved(jnp.concatenate([wide1[1:], wide2[1:]], axis=0), ROW, 1)

    def rows_of(above, wide, k):
        both = jnp.concatenate([above, wide], axis=0)
        start = tile - 2 - offsets[k, 0]
        return lax.dynamic_slice(both, (start, jnp.int32(0), jnp.int32(0)), (ext, ext_cols, width)) * inside

    joined = jnp.stack(
        [
            jnp.concatenate([side[:, cols + 4 :], cot, right[:, 1:]], axis=1),
            jnp.concatenate([side[:, cols + 3 : cols + 4], now, right[:, :1]], axis=1),
            jnp.concatenate([side[:, cols : cols + 3], near0[:, : cols - 1]], axis=1) * inside,
            rows_of(above12[: tile - 1], wide1, 1),
            rows_of(above12[tile - 1 :], wide2, 2),
            jnp.concatenate([side[:, 1:cols], near3[:, :3]], axis=1) * inside,
        ]
    )
    hidden, back_pre = forward(
        joined, merge_weight.reshape(9, -1, width), out_weight.reshape(9, width, width)
    )
    first = core[0] == 0

    def swapped(x):
        return lax.ppermute(x, "core", SWAP)

    flat_cot = cotangent.reshape(tile * cols, width)
    other_two = swapped(jnp.where(first, joined[4:6], joined[1:3]))

    hidden = hidden.reshape(tile, cols, width)
    hidden_above = moved(hidden[-1:], ROW, 1)
    hidden_below = moved(hidden[:1], ROW, -1)
    other_back = swapped(back_pre)
    at = jnp.concatenate([3 * core + 1, jnp.zeros((1,), jnp.int32)])
    sums = layer_gradient(0, at, joined, other_two, back_pre, other_back)
    sums, hidden_above, hidden_below, flat_cot = lax.optimization_barrier(
        (sums, hidden_above, hidden_below, flat_cot)
    )
    other_cot = swapped(flat_cot)
    hidden_pad = jnp.concatenate([hidden_above, hidden, hidden_below], axis=0)
    hidden_left = moved(hidden_pad[:, -1:], COL, 1)
    hidden_right = moved(hidden_pad[:, :1], COL, -1)
    sums = layer_gradient(1, at + 1, joined, other_two, back_pre, other_back, (sums,))
    sums, hidden_left, hidden_right = lax.optimization_barrier((sums, hidden_left, hidden_right))
    hidden_pad = jnp.concatenate([hidden_left, hidden_pad, hidden_right], axis=1)
    own_third = jnp.where(first, joined[3], hidden_pad)
    other_third = swapped(jnp.where(first, hidden_pad, joined[3]))
    sums = layer_gradient(
        2,
        jnp.zeros((2,), jnp.int32),
        own_third[None],
        other_third[None],
        jnp.where(first, back_pre, flat_cot),
        jnp.where(first, other_back, other_cot),
        (sums,),
    )
    merged = merged_step(hidden_pad, current, out_weight.reshape(9, width, width))

    chips = lax.axis_size(CHIPS)
    half = width // 2
    blocks = sums.reshape(chips, -1, half)
    got = lax.all_to_all(blocks, CHIPS, split_axis=0, concat_axis=0)
    got, merged = lax.optimization_barrier((got, merged))
    share = jnp.sum(got.astype(F32), axis=0).astype(BF16)
    spread = jnp.broadcast_to(share[None], blocks.shape)
    own = lax.all_to_all(spread, CHIPS, split_axis=0, concat_axis=0).reshape(sums.shape)
    other = swapped(own)
    merge_grad = final(3 * (1 - core), other, (final(3 * core, own),))
    merge_grad = merge_grad.reshape(merge_weight.shape)
    third = jnp.where(first, other[2], own[2])
    out_grad = jnp.concatenate([third[0], third[1]], axis=1).astype(F32).reshape(out_weight.shape)
    return (merged, merge_grad, out_grad)


def solution(mesh):
    parts = Mesh(mesh.devices.reshape(2, 2, 2, 4, 4), ("xh", "core", "xl", "z", "y"))
    return jax.shard_map(
        shards,
        mesh=parts,
        in_specs=(
            P(ROW, COL, None),
            P(None, ROW, COL, None),
            P(None, ROW, COL),
            P(),
            P(),
            P(),
            P(ROW, COL, None),
        ),
        out_specs=(P(ROW, COL, None), P(), P()),
        check_vma=False,
    )
```

```python
import functools

import jax
import jax.numpy as jnp
from jax import lax
from jax.experimental import pallas as pl
from jax.experimental.pallas import tpu as pltpu
from jax.sharding import Mesh, PartitionSpec as P

CHIPS = ("xh", "xl", "z", "y")
ROW = ("xh", "core")
COL = ("xl", "z", "y")
BF16 = jnp.bfloat16
F32 = jnp.float32
SWAP = [(0, 1), (1, 0)]


def work(products, moved_bytes):
    return pl.CostEstimate(flops=2 * products, transcendentals=0, bytes_accessed=moved_bytes)


PARAMS = pltpu.CompilerParams(
    dimension_semantics=("arbitrary",), vmem_limit_bytes=56 * 1024 * 1024
)
WHOLE = pl.BlockSpec(memory_space=pltpu.VMEM)


def moved(x, axis, by):
    peers = lax.axis_size(axis)
    return lax.ppermute(x, axis, [(i, i + by) for i in range(peers) if 0 <= i + by < peers])


def shift_row(value, row, target):
    cols = target.shape[2]
    wide = value.astype(F32)
    target[0, row] = value[:cols]
    for col_step in (1, 2):
        target[col_step, row] = wide[col_step : col_step + cols].astype(BF16)


def forward_kernel(joined_ref, weight_ref, out_weight_ref, hidden_ref, back_ref, even, odd, total,
                   back_total):
    step = pl.program_id(0)
    steps = pl.num_programs(0)
    _, rows, cols, width = even.shape
    tile = rows - 2

    def taps(now, before, shifting, multiply):
        def tap(t, carry):
            if multiply is not None:
                multiply(t, before)
            if shifting:
                for more in range(4):
                    row = jnp.minimum(4 * t + more, rows - 1)
                    shift_row(joined_ref[0, row], row, now)
            return carry

        lax.fori_loop(0, 9, tap, 0, unroll=True)

    def forward_tap(t, before):
        window = before[t % 3, pl.ds(t // 3, tile)].reshape(tile * cols, width)
        total[...] += jnp.dot(window, weight_ref[t], preferred_element_type=F32)

    def back_tap(t, before):
        window = before[2 - t % 3, pl.ds(2 - t // 3, tile)].reshape(tile * cols, width)
        back_total[...] += lax.dot_general(
            window, out_weight_ref[t], (((1,), (1,)), ((), ())), preferred_element_type=F32
        )

    @pl.when(step == 0)
    def _():
        total[...] = jnp.zeros_like(total)
        back_total[...] = jnp.zeros_like(back_total)
        taps(even, odd, True, None)

    @pl.when(step == 1)
    def _():
        taps(odd, even, True, back_tap)

    @pl.when((step > 1) & (step < steps - 1) & (step % 2 == 0))
    def _():
        taps(even, odd, True, forward_tap)

    @pl.when((step > 1) & (step < steps - 1) & (step % 2 == 1))
    def _():
        taps(odd, even, True, forward_tap)

    @pl.when(step == steps - 1)
    def _():
        taps(even, odd, False, forward_tap)
        pre = total[...]
        sigma = jax.nn.sigmoid(pre)
        hidden_ref[...] = (pre * sigma).astype(BF16)
        back = back_total[...] * (sigma * (1.0 + pre * (1.0 - sigma)))
        back_ref[...] = back.astype(BF16)


def forward(joined, cols, merge_weight, out_weight):
    layers, rows, _, width = joined.shape
    frames = layers - 1
    cells = (rows - 2) * cols
    return pl.pallas_call(
        forward_kernel,
        grid=(layers + 1,),
        in_specs=[
            pl.BlockSpec((1,) + joined.shape[1:], lambda i: (jnp.minimum(i, frames), 0, 0, 0)),
            pl.BlockSpec((9, width, width), lambda i: (0, jnp.maximum(i - 2, 0), 0)),
            pl.BlockSpec((9, width, width), lambda i: (0, 0, 0)),
        ],
        out_specs=[
            pl.BlockSpec((cells, width), lambda i: (0, 0)),
            pl.BlockSpec((cells, width), lambda i: (0, 0)),
        ],
        out_shape=[
            jax.ShapeDtypeStruct((cells, width), BF16),
            jax.ShapeDtypeStruct((cells, width), BF16),
        ],
        scratch_shapes=[
            pltpu.VMEM((3, rows, cols, width), BF16),
            pltpu.VMEM((3, rows, cols, width), BF16),
            pltpu.VMEM((cells, width), F32),
            pltpu.VMEM((cells, width), F32),
        ],
        compiler_params=PARAMS,
        cost_estimate=work(9 * cells * width * width * layers, 25_000_000),
        name="forward",
    )(joined, merge_weight, out_weight)


def layer_taps(own_row, other_row, own_right, other_right, out_ref, own_copies, other_copies, held):
    _, rows, cols, width = own_copies.shape
    tile, half = rows - 2, width // 2

    def product(copies, tap, right):
        window = copies[tap % 3, tap // 3 : tap // 3 + tile].reshape(tile * cols, width)
        return lax.dot_general(
            window, right[...], (((0,), (0,)), ((), ())), preferred_element_type=F32
        )

    for row in range(rows):
        shift_row(own_row(row), row, own_copies)
    for tap in range(9):
        held[tap] = product(own_copies, tap, own_right)
        for row in range(4 * tap, min(4 * tap + 4, rows)):
            shift_row(other_row(row), row, other_copies)
    for tap in range(9):
        value = held[tap] + product(other_copies, tap, other_right)
        for side in range(2):
            part = value[:, side * half : (side + 1) * half]
            out_ref[0, side, tap * width : (tap + 1) * width] = part.astype(BF16)


def layer_kernel(core_ref, own_ref, other_ref, own_right, other_right, *refs):
    layer_taps(
        lambda row: own_ref[0, row], lambda row: other_ref[0, row], own_right, other_right, *refs[-4:]
    )


def third_kernel(core_ref, own_ref, other_ref, own_hidden, other_hidden, own_back, other_back, own_cot,
                 other_cot, into_ref, out_ref, own_copies, other_copies, held, own_right, other_right):
    first = core_ref[0] == 0
    own_right[...] = jnp.where(first, own_back[...], own_cot[...])
    other_right[...] = jnp.where(first, other_back[...], other_cot[...])
    layer_taps(
        lambda row: jnp.where(first, own_ref[0, row], own_hidden[row]),
        lambda row: jnp.where(first, other_ref[0, row], other_hidden[row]),
        own_right,
        other_right,
        out_ref,
        own_copies,
        other_copies,
        held,
    )


def layer_gradient(place, core, cols, windows, hidden, rights, into=()):
    _, rows, wide_cols, width = windows[0].shape
    shape = (3, 2, 9 * width, width // 2)
    cells = (rows - 2) * cols
    if hidden:
        layer = pl.BlockSpec((1, rows, wide_cols, width), lambda i, at: (3, 0, 0, 0))
    else:
        layer = pl.BlockSpec(
            (1, rows, wide_cols, width), lambda i, at: (3 * at[0] + 1 + place, 0, 0, 0)
        )
    whole = pl.BlockSpec((rows, wide_cols, width), lambda i, at: (0, 0, 0))
    right = pl.BlockSpec((cells, width), lambda i, at: (0, 0))
    operands = (core, *windows, *hidden, *rights, *into)
    more = [pltpu.VMEM((cells, width), BF16)] * 2 if hidden else []
    return pl.pallas_call(
        third_kernel if hidden else layer_kernel,
        grid_spec=pltpu.PrefetchScalarGridSpec(
            num_scalar_prefetch=1,
            grid=(1,),
            in_specs=[layer] * 2
            + [whole] * len(hidden)
            + [right] * len(rights)
            + [pl.BlockSpec(memory_space=pl.ANY)] * len(into),
            out_specs=pl.BlockSpec((1,) + shape[1:], lambda i, at: (place, 0, 0, 0)),
            scratch_shapes=[
                pltpu.VMEM((3, rows, cols, width), BF16),
                pltpu.VMEM((3, rows, cols, width), BF16),
                pltpu.VMEM((9, width, width), F32),
            ]
            + more,
        ),
        out_shape=jax.ShapeDtypeStruct(shape, BF16),
        input_output_aliases={len(operands) - 1: 0} if into else {},
        compiler_params=PARAMS,
        cost_estimate=work(18 * cells * width * width, 5_000_000),
        name="layer_gradient",
    )(*operands)


def merged_kernel(hidden_ref, current_ref, weight_ref, merged_ref, copies, total):
    _, rows, cols, width = copies.shape
    tile = rows - 2
    for row in range(rows):
        shift_row(hidden_ref[row], row, copies)
    total[...] = current_ref[...].reshape(tile * cols, width).astype(F32)
    for tap in range(9):
        window = copies[tap % 3, tap // 3 : tap // 3 + tile].reshape(tile * cols, width)
        total[...] += jnp.dot(window, weight_ref[tap], preferred_element_type=F32)
    merged_ref[...] = total[...].astype(BF16).reshape(merged_ref.shape)


def merged_step(hidden_pad, current, out_weight):
    tile, cols, width = current.shape
    whole = [pl.BlockSpec(x.shape, lambda i: (0, 0, 0)) for x in (hidden_pad, current, out_weight)]
    return pl.pallas_call(
        merged_kernel,
        grid=(1,),
        in_specs=whole,
        out_specs=whole[1],
        out_shape=jax.ShapeDtypeStruct(current.shape, BF16),
        scratch_shapes=[
            pltpu.VMEM((3, tile + 2, cols, width), BF16),
            pltpu.VMEM((tile * cols, width), F32),
        ],
        compiler_params=PARAMS,
        cost_estimate=work(9 * tile * cols * width * width, 4_000_000),
        name="merged_step",
    )(hidden_pad, current, out_weight)


def final_kernel(base_ref, sums_ref, *refs):
    out_ref = refs[-1]
    taps, width, _ = out_ref.shape
    half = sums_ref.shape[-1]

    @pl.when(base_ref[0] + pl.program_id(0) < 5)
    def _():
        for side in range(2):
            part = sums_ref[0, side].reshape(taps, width, half)
            out_ref[:, :, side * half : (side + 1) * half] = part.astype(F32)


def final(base, sums, into=()):
    width = 2 * sums.shape[-1]
    return pl.pallas_call(
        final_kernel,
        grid_spec=pltpu.PrefetchScalarGridSpec(
            num_scalar_prefetch=1,
            grid=(3,),
            in_specs=[pl.BlockSpec((1,) + sums.shape[1:], lambda i, at: (i, 0, 0, 0))]
            + [pl.BlockSpec(memory_space=pl.ANY)] * len(into),
            out_specs=pl.BlockSpec(
                (9, width, width), lambda i, at: (0, jnp.minimum(at[0] + i, 4), 0)
            ),
        ),
        out_shape=jax.ShapeDtypeStruct((9, 5 * width, width), F32),
        input_output_aliases={2: 0} if into else {},
        compiler_params=PARAMS,
        cost_estimate=work(0, 12_000_000),
        name="final",
    )(base, sums, *into)


def shards(current, history, validity, offsets, merge_weight, out_weight, cotangent):
    tile, cols, width = current.shape
    frames = history.shape[0]
    ext = tile + 2
    core = lax.axis_index("core").astype(jnp.int32).reshape(1)
    valid = validity.astype(BF16)[..., None]
    masked12 = history[1:3] * valid[1:3]
    masked12, valid = lax.optimization_barrier((masked12, valid))
    masked = [history[0] * valid[0], masked12[0], masked12[1], history[3] * valid[3]]

    row_last = lax.axis_index(ROW) == lax.axis_size(ROW) - 1
    col_last = lax.axis_index(COL) == lax.axis_size(COL) - 1
    row_inside = (jnp.arange(ext) < ext - 1) | ~row_last
    ext_cols = cols + 2
    col_inside = (jnp.arange(ext_cols) < ext_cols - 1) | ~col_last
    inside = (row_inside[:, None] & col_inside[None, :]).astype(BF16)[..., None]

    left12 = moved(masked12, COL, 1)
    packed = moved(
        jnp.concatenate([masked[3][1:], masked[0][-3:], current[-1:], cotangent[-1:]], axis=0), ROW, 1
    )
    below = moved(jnp.concatenate([current[:1], cotangent[:1]], axis=0), ROW, -1)
    above3, above0 = packed[: tile - 1], packed[tile - 1 : tile + 2]
    near3 = jnp.concatenate([above3, masked[3][:3]], axis=0)
    near0 = jnp.concatenate([above0, masked[0][: tile - 1]], axis=0)
    now = jnp.concatenate([packed[tile + 2 : tile + 3], current, below[:1]], axis=0)
    cot = jnp.concatenate([packed[tile + 3 :], cotangent, below[1:]], axis=0)
    side = moved(
        jnp.concatenate([near3, near0[:, -3:], now[:, -1:], cot[:, -1:]], axis=1), COL, 1
    )
    right = moved(jnp.concatenate([now[:, :1], cot[:, :1]], axis=1), COL, -1)

    left12, right = lax.optimization_barrier((left12, right))

    def cols_of(k):
        wide = jnp.concatenate([left12[k - 1], masked[k]], axis=1)
        start = cols - 1 - offsets[k, 1]
        return lax.dynamic_slice(wide, (jnp.int32(0), start, jnp.int32(0)), (tile, ext_cols, width))

    wide1, wide2 = cols_of(1), cols_of(2)
    above12 = moved(jnp.concatenate([wide1[1:], wide2[1:]], axis=0), ROW, 1)

    def rows_of(above, wide, k):
        both = jnp.concatenate([above, wide], axis=0)
        start = tile - 2 - offsets[k, 0]
        return lax.dynamic_slice(both, (start, jnp.int32(0), jnp.int32(0)), (ext, ext_cols, width)) * inside

    blank = jnp.zeros((ext, -ext_cols % 8, width), BF16)

    def filled(*pieces):
        return jnp.concatenate([*pieces, blank], axis=1)

    joined = jnp.stack(
        [
            filled(side[:, cols + 4 :], cot, right[:, 1:]),
            filled(side[:, cols + 3 : cols + 4], now, right[:, :1]),
            filled(jnp.concatenate([side[:, cols : cols + 3], near0[:, : cols - 1]], axis=1) * inside),
            filled(rows_of(above12[: tile - 1], wide1, 1)),
            filled(rows_of(above12[tile - 1 :], wide2, 2)),
            filled(jnp.concatenate([side[:, 1:cols], near3[:, :3]], axis=1) * inside),
        ]
    )
    hidden, back_pre = forward(
        joined, cols, merge_weight.reshape(9, -1, width), out_weight.reshape(9, width, width)
    )
    first = core[0] == 0

    def swapped(x):
        return lax.ppermute(x, "core", SWAP)

    flat_cot = cotangent.reshape(tile * cols, width)
    windows = (joined, swapped(joined))

    hidden = hidden.reshape(tile, cols, width)
    hidden_above = moved(hidden[-1:], ROW, 1)
    hidden_below = moved(hidden[:1], ROW, -1)
    backs = (back_pre, swapped(back_pre))
    sums = layer_gradient(0, core, cols, windows, (), backs)
    sums, hidden_above, hidden_below, flat_cot = lax.optimization_barrier(
        (sums, hidden_above, hidden_below, flat_cot)
    )
    other_cot = swapped(flat_cot)
    hidden_pad = jnp.concatenate([hidden_above, hidden, hidden_below], axis=0)
    hidden_left = moved(hidden_pad[:, -1:], COL, 1)
    hidden_right = moved(hidden_pad[:, :1], COL, -1)
    sums = layer_gradient(1, core, cols, windows, (), backs, (sums,))
    sums, hidden_left, hidden_right, other_cot = lax.optimization_barrier(
        (sums, hidden_left, hidden_right, other_cot)
    )
    cots = (flat_cot, other_cot)
    hidden_pad = filled(hidden_left, hidden_pad, hidden_right)
    hiddens = (hidden_pad, swapped(hidden_pad))
    sums = layer_gradient(2, core, cols, windows, hiddens, (*backs, *cots), (sums,))
    merged = merged_step(hidden_pad, current, out_weight.reshape(9, width, width))

    chips = lax.axis_size(CHIPS)
    half = width // 2
    blocks = sums.reshape(chips, -1, half)
    got = lax.all_to_all(blocks, CHIPS, split_axis=0, concat_axis=0)
    share = jnp.sum(got.astype(F32), axis=0).astype(BF16)
    spread = jnp.broadcast_to(share[None], blocks.shape)
    own = lax.all_to_all(spread, CHIPS, split_axis=0, concat_axis=0).reshape(sums.shape)
    other = swapped(own)
    merge_grad = final(3 * (1 - core), other, (final(3 * core, own),))
    merge_grad = merge_grad.reshape(merge_weight.shape)
    third = jnp.where(first, other[2], own[2])
    out_grad = jnp.concatenate([third[0], third[1]], axis=1).astype(F32).reshape(out_weight.shape)
    return (merged, merge_grad, out_grad)


def solution(mesh):
    parts = Mesh(mesh.devices.reshape(2, 2, 2, 4, 4), ("xh", "core", "xl", "z", "y"))
    return jax.shard_map(
        shards,
        mesh=parts,
        in_specs=(
            P(ROW, COL, None),
            P(None, ROW, COL, None),
            P(None, ROW, COL),
            P(),
            P(),
            P(),
            P(ROW, COL, None),
        ),
        out_specs=(P(ROW, COL, None), P(), P()),
        check_vma=False,
    )
```

```python
import functools

import jax
import jax.numpy as jnp
from jax import lax
from jax.experimental import pallas as pl
from jax.experimental.pallas import tpu as pltpu
from jax.sharding import Mesh, PartitionSpec as P

CHIPS = ("xh", "xl", "z", "y")
ROW = ("xh", "core")
COL = ("xl", "z", "y")
BF16 = jnp.bfloat16
F32 = jnp.float32
SWAP = [(0, 1), (1, 0)]


def work(products, moved_bytes):
    return pl.CostEstimate(flops=2 * products, transcendentals=0, bytes_accessed=moved_bytes)


PARAMS = pltpu.CompilerParams(
    dimension_semantics=("arbitrary",), vmem_limit_bytes=56 * 1024 * 1024
)
WHOLE = pl.BlockSpec(memory_space=pltpu.VMEM)


def moved(x, axis, by):
    peers = lax.axis_size(axis)
    return lax.ppermute(x, axis, [(i, i + by) for i in range(peers) if 0 <= i + by < peers])


def shift_row(value, row, target):
    cols = target.shape[2]
    wide = value.astype(F32)
    target[0, row] = value[:cols]
    for col_step in (1, 2):
        target[col_step, row] = wide[col_step : col_step + cols].astype(BF16)


def forward_kernel(joined_ref, weight_ref, out_weight_ref, hidden_ref, back_ref, even, odd, total,
                   back_total):
    step = pl.program_id(0)
    steps = pl.num_programs(0)
    _, rows, cols, width = even.shape
    tile = rows - 2

    def taps(now, before, shifting, multiply):
        def tap(t, carry):
            if multiply is not None:
                multiply(t, before)
            if shifting:
                for more in range(4):
                    row = jnp.minimum(4 * t + more, rows - 1)
                    shift_row(joined_ref[0, row], row, now)
            return carry

        lax.fori_loop(0, 9, tap, 0, unroll=True)

    def forward_tap(t, before):
        window = before[t % 3, pl.ds(t // 3, tile)].reshape(tile * cols, width)
        total[...] += jnp.dot(window, weight_ref[t], preferred_element_type=F32)

    def back_tap(t, before):
        window = before[2 - t % 3, pl.ds(2 - t // 3, tile)].reshape(tile * cols, width)
        back_total[...] += lax.dot_general(
            window, out_weight_ref[t], (((1,), (1,)), ((), ())), preferred_element_type=F32
        )

    @pl.when(step == 0)
    def _():
        total[...] = jnp.zeros_like(total)
        back_total[...] = jnp.zeros_like(back_total)
        taps(even, odd, True, None)

    @pl.when(step == 1)
    def _():
        taps(odd, even, True, back_tap)

    @pl.when((step > 1) & (step < steps - 1) & (step % 2 == 0))
    def _():
        taps(even, odd, True, forward_tap)

    @pl.when((step > 1) & (step < steps - 1) & (step % 2 == 1))
    def _():
        taps(odd, even, True, forward_tap)

    @pl.when(step == steps - 1)
    def _():
        taps(even, odd, False, forward_tap)
        pre = total[...]
        sigma = jax.nn.sigmoid(pre)
        hidden_ref[...] = (pre * sigma).astype(BF16)
        back = back_total[...] * (sigma * (1.0 + pre * (1.0 - sigma)))
        back_ref[...] = back.astype(BF16)


def forward(joined, cols, merge_weight, out_weight):
    layers, rows, _, width = joined.shape
    frames = layers - 1
    cells = (rows - 2) * cols
    return pl.pallas_call(
        forward_kernel,
        grid=(layers + 1,),
        in_specs=[
            pl.BlockSpec((1,) + joined.shape[1:], lambda i: (jnp.minimum(i, frames), 0, 0, 0)),
            pl.BlockSpec((9, width, width), lambda i: (0, jnp.maximum(i - 2, 0), 0)),
            pl.BlockSpec((9, width, width), lambda i: (0, 0, 0)),
        ],
        out_specs=[
            pl.BlockSpec((cells, width), lambda i: (0, 0)),
            pl.BlockSpec((cells, width), lambda i: (0, 0)),
        ],
        out_shape=[
            jax.ShapeDtypeStruct((cells, width), BF16),
            jax.ShapeDtypeStruct((cells, width), BF16),
        ],
        scratch_shapes=[
            pltpu.VMEM((3, rows, cols, width), BF16),
            pltpu.VMEM((3, rows, cols, width), BF16),
            pltpu.VMEM((cells, width), F32),
            pltpu.VMEM((cells, width), F32),
        ],
        compiler_params=PARAMS,
        cost_estimate=work(9 * cells * width * width * layers, 25_000_000),
        name="forward",
    )(joined, merge_weight, out_weight)


def layer_taps(own_row, other_row, own_right, other_right, out_ref, own_copies, other_copies, held):
    _, rows, cols, width = own_copies.shape
    tile, half = rows - 2, width // 2

    def product(copies, tap, right):
        window = copies[tap % 3, tap // 3 : tap // 3 + tile].reshape(tile * cols, width)
        return lax.dot_general(
            window, right[...], (((0,), (0,)), ((), ())), preferred_element_type=F32
        )

    for row in range(rows):
        shift_row(own_row(row), row, own_copies)
    for tap in range(9):
        held[tap] = product(own_copies, tap, own_right)
        for row in range(4 * tap, min(4 * tap + 4, rows)):
            shift_row(other_row(row), row, other_copies)
    for tap in range(9):
        value = held[tap] + product(other_copies, tap, other_right)
        for side in range(2):
            part = value[:, side * half : (side + 1) * half]
            out_ref[0, side, tap * width : (tap + 1) * width] = part.astype(BF16)


def layer_kernel(core_ref, own_ref, other_ref, own_right, other_right, *refs):
    layer_taps(
        lambda row: own_ref[0, row], lambda row: other_ref[0, row], own_right, other_right, *refs[-4:]
    )


def third_kernel(core_ref, own_ref, other_ref, own_hidden, other_hidden, own_back, other_back, own_cot,
                 other_cot, into_ref, out_ref, own_copies, other_copies, held, own_right, other_right):
    first = core_ref[0] == 0
    own_right[...] = jnp.where(first, own_back[...], own_cot[...])
    other_right[...] = jnp.where(first, other_back[...], other_cot[...])
    layer_taps(
        lambda row: jnp.where(first, own_ref[0, row], own_hidden[row]),
        lambda row: jnp.where(first, other_ref[0, row], other_hidden[row]),
        own_right,
        other_right,
        out_ref,
        own_copies,
        other_copies,
        held,
    )


def layer_gradient(place, core, cols, windows, hidden, rights, into=()):
    _, rows, wide_cols, width = windows[0].shape
    shape = (3, 2, 9 * width, width // 2)
    cells = (rows - 2) * cols
    if hidden:
        layer = pl.BlockSpec((1, rows, wide_cols, width), lambda i, at: (3, 0, 0, 0))
    else:
        layer = pl.BlockSpec(
            (1, rows, wide_cols, width), lambda i, at: (3 * at[0] + 1 + place, 0, 0, 0)
        )
    whole = pl.BlockSpec((rows, wide_cols, width), lambda i, at: (0, 0, 0))
    right = pl.BlockSpec((cells, width), lambda i, at: (0, 0))
    operands = (core, *windows, *hidden, *rights, *into)
    more = [pltpu.VMEM((cells, width), BF16)] * 2 if hidden else []
    return pl.pallas_call(
        third_kernel if hidden else layer_kernel,
        grid_spec=pltpu.PrefetchScalarGridSpec(
            num_scalar_prefetch=1,
            grid=(1,),
            in_specs=[layer] * 2
            + [whole] * len(hidden)
            + [right] * len(rights)
            + [pl.BlockSpec(memory_space=pl.ANY)] * len(into),
            out_specs=pl.BlockSpec((1,) + shape[1:], lambda i, at: (place, 0, 0, 0)),
            scratch_shapes=[
                pltpu.VMEM((3, rows, cols, width), BF16),
                pltpu.VMEM((3, rows, cols, width), BF16),
                pltpu.VMEM((9, width, width), F32),
            ]
            + more,
        ),
        out_shape=jax.ShapeDtypeStruct(shape, BF16),
        input_output_aliases={len(operands) - 1: 0} if into else {},
        compiler_params=PARAMS,
        cost_estimate=work(18 * cells * width * width, 5_000_000),
        name="layer_gradient",
    )(*operands)


def merged_kernel(hidden_ref, current_ref, weight_ref, merged_ref, copies, total):
    _, rows, cols, width = copies.shape
    tile = rows - 2
    for row in range(rows):
        shift_row(hidden_ref[row], row, copies)
    total[...] = current_ref[...].reshape(tile * cols, width).astype(F32)
    for tap in range(9):
        window = copies[tap % 3, tap // 3 : tap // 3 + tile].reshape(tile * cols, width)
        total[...] += jnp.dot(window, weight_ref[tap], preferred_element_type=F32)
    merged_ref[...] = total[...].astype(BF16).reshape(merged_ref.shape)


def merged_step(hidden_pad, current, out_weight):
    tile, cols, width = current.shape
    whole = [pl.BlockSpec(x.shape, lambda i: (0, 0, 0)) for x in (hidden_pad, current, out_weight)]
    return pl.pallas_call(
        merged_kernel,
        grid=(1,),
        in_specs=whole,
        out_specs=whole[1],
        out_shape=jax.ShapeDtypeStruct(current.shape, BF16),
        scratch_shapes=[
            pltpu.VMEM((3, tile + 2, cols, width), BF16),
            pltpu.VMEM((tile * cols, width), F32),
        ],
        compiler_params=PARAMS,
        cost_estimate=work(9 * tile * cols * width * width, 4_000_000),
        name="merged_step",
    )(hidden_pad, current, out_weight)


def final_kernel(base_ref, sums_ref, *refs):
    out_ref = refs[-1]
    taps, width, _ = out_ref.shape
    half = sums_ref.shape[-1]

    @pl.when(base_ref[0] + pl.program_id(0) < 5)
    def _():
        for side in range(2):
            part = sums_ref[0, side].reshape(taps, width, half)
            out_ref[:, :, side * half : (side + 1) * half] = part.astype(F32)


def final(base, sums, into=()):
    width = 2 * sums.shape[-1]
    return pl.pallas_call(
        final_kernel,
        grid_spec=pltpu.PrefetchScalarGridSpec(
            num_scalar_prefetch=1,
            grid=(3,),
            in_specs=[pl.BlockSpec((1,) + sums.shape[1:], lambda i, at: (i, 0, 0, 0))]
            + [pl.BlockSpec(memory_space=pl.ANY)] * len(into),
            out_specs=pl.BlockSpec(
                (9, width, width), lambda i, at: (0, jnp.minimum(at[0] + i, 4), 0)
            ),
        ),
        out_shape=jax.ShapeDtypeStruct((9, 5 * width, width), F32),
        input_output_aliases={2: 0} if into else {},
        compiler_params=PARAMS,
        cost_estimate=work(0, 12_000_000),
        name="final",
    )(base, sums, *into)


def shards(current, history, validity, offsets, merge_weight, out_weight, cotangent):
    tile, cols, width = current.shape
    frames = history.shape[0]
    ext = tile + 2
    core = lax.axis_index("core").astype(jnp.int32).reshape(1)
    valid = validity.astype(BF16)[..., None]
    masked = [history[k] * valid[k] for k in range(frames)]

    row_last = lax.axis_index(ROW) == lax.axis_size(ROW) - 1
    col_last = lax.axis_index(COL) == lax.axis_size(COL) - 1
    row_inside = (jnp.arange(ext) < ext - 1) | ~row_last
    ext_cols = cols + 2
    col_inside = (jnp.arange(ext_cols) < ext_cols - 1) | ~col_last
    inside = (row_inside[:, None] & col_inside[None, :]).astype(BF16)[..., None]

    packed = moved(
        jnp.concatenate(
            [masked[3][1:], masked[2][1:], masked[0][-3:], current[-1:], cotangent[-1:]], axis=0
        ),
        ROW,
        1,
    )
    left1 = moved(masked[1], COL, 1)
    below = moved(jnp.concatenate([current[:1], cotangent[:1]], axis=0), ROW, -1)
    above3, above2, rest = packed[: tile - 1], packed[tile - 1 : 2 * tile - 2], packed[2 * tile - 2 :]

    def rows_of(above, window, k):
        both = jnp.concatenate([above, window], axis=0)
        start = (tile - 2 - offsets[k, 0], jnp.int32(0), jnp.int32(0))
        return lax.dynamic_slice(both, start, (ext,) + window.shape[1:])

    def cols_of(left, window, k):
        both = jnp.concatenate([left, window], axis=1)
        start = (jnp.int32(0), cols - 1 - offsets[k, 1], jnp.int32(0))
        return lax.dynamic_slice(both, start, (window.shape[0], ext_cols, width))

    near3 = jnp.concatenate([above3, masked[3][:3]], axis=0)
    near2 = rows_of(above2, masked[2], 2)
    near0 = jnp.concatenate([rest[:3], masked[0][: tile - 1]], axis=0)
    now = jnp.concatenate([rest[3:4], current, below[:1]], axis=0)
    cot = jnp.concatenate([rest[4:], cotangent, below[1:]], axis=0)
    rims = jnp.concatenate([near0[:, -3:], now[:, -1:], cot[:, -1:]], axis=1)
    side = moved(jnp.concatenate([near3, near2, rims], axis=1), COL, 1)
    left3, left2, rims = side[:, :cols], side[:, cols : 2 * cols], side[:, 2 * cols :]
    right = moved(jnp.concatenate([now[:, :1], cot[:, :1]], axis=1), COL, -1)
    left1, right = lax.optimization_barrier((left1, right))
    wide1 = cols_of(left1, masked[1], 1)
    above1 = moved(wide1[1:], ROW, 1)

    blank = jnp.zeros((ext, -ext_cols % 8, width), BF16)

    def filled(*pieces):
        return jnp.concatenate([*pieces, blank], axis=1)

    joined = jnp.stack(
        [
            filled(rims[:, 4:], cot, right[:, 1:]),
            filled(rims[:, 3:4], now, right[:, :1]),
            filled(jnp.concatenate([rims[:, :3], near0[:, : cols - 1]], axis=1) * inside),
            filled(rows_of(above1, wide1, 1) * inside),
            filled(cols_of(left2, near2, 2) * inside),
            filled(jnp.concatenate([left3[:, 1:], near3[:, :3]], axis=1) * inside),
        ]
    )
    hidden, back_pre = forward(
        joined, cols, merge_weight.reshape(9, -1, width), out_weight.reshape(9, width, width)
    )
    first = core[0] == 0

    def swapped(x):
        return lax.ppermute(x, "core", SWAP)

    flat_cot = cotangent.reshape(tile * cols, width)
    windows = (joined, swapped(joined))

    hidden = hidden.reshape(tile, cols, width)
    hidden_above = moved(hidden[-1:], ROW, 1)
    hidden_below = moved(hidden[:1], ROW, -1)
    backs = (back_pre, swapped(back_pre))
    sums = layer_gradient(0, core, cols, windows, (), backs)
    sums, hidden_above, hidden_below, flat_cot = lax.optimization_barrier(
        (sums, hidden_above, hidden_below, flat_cot)
    )
    other_cot = swapped(flat_cot)
    hidden_pad = jnp.concatenate([hidden_above, hidden, hidden_below], axis=0)
    hidden_left = moved(hidden_pad[:, -1:], COL, 1)
    hidden_right = moved(hidden_pad[:, :1], COL, -1)
    sums = layer_gradient(1, core, cols, windows, (), backs, (sums,))
    sums, hidden_left, hidden_right, other_cot = lax.optimization_barrier(
        (sums, hidden_left, hidden_right, other_cot)
    )
    cots = (flat_cot, other_cot)
    hidden_pad = filled(hidden_left, hidden_pad, hidden_right)
    hiddens = (hidden_pad, swapped(hidden_pad))
    sums = layer_gradient(2, core, cols, windows, hiddens, (*backs, *cots), (sums,))
    merged = merged_step(hidden_pad, current, out_weight.reshape(9, width, width))

    chips = lax.axis_size(CHIPS)
    half = width // 2
    blocks = sums.reshape(chips, -1, half)
    got = lax.all_to_all(blocks, CHIPS, split_axis=0, concat_axis=0)
    share = jnp.sum(got.astype(F32), axis=0).astype(BF16)
    spread = jnp.broadcast_to(share[None], blocks.shape)
    own = lax.all_to_all(spread, CHIPS, split_axis=0, concat_axis=0).reshape(sums.shape)
    other = swapped(own)
    merge_grad = final(3 * (1 - core), other, (final(3 * core, own),))
    merge_grad = merge_grad.reshape(merge_weight.shape)
    third = jnp.where(first, other[2], own[2])
    out_grad = jnp.concatenate([third[0], third[1]], axis=1).astype(F32).reshape(out_weight.shape)
    return (merged, merge_grad, out_grad)


def solution(mesh):
    parts = Mesh(mesh.devices.reshape(2, 2, 2, 4, 4), ("xh", "core", "xl", "z", "y"))
    return jax.shard_map(
        shards,
        mesh=parts,
        in_specs=(
            P(ROW, COL, None),
            P(None, ROW, COL, None),
            P(None, ROW, COL),
            P(),
            P(),
            P(),
            P(ROW, COL, None),
        ),
        out_specs=(P(ROW, COL, None), P(), P()),
        check_vma=False,
    )
```

```python
import functools

import jax
import jax.numpy as jnp
from jax import lax
from jax.experimental import pallas as pl
from jax.experimental.pallas import tpu as pltpu
from jax.sharding import Mesh, PartitionSpec as P

CHIPS = ("xh", "xl", "z", "y")
ROW = ("xh", "core")
COL = ("xl", "z", "y")
BF16 = jnp.bfloat16
F32 = jnp.float32
SWAP = [(0, 1), (1, 0)]


def work(products, moved_bytes):
    return pl.CostEstimate(flops=2 * products, transcendentals=0, bytes_accessed=moved_bytes)


PARAMS = pltpu.CompilerParams(
    dimension_semantics=("arbitrary",), vmem_limit_bytes=56 * 1024 * 1024
)
WHOLE = pl.BlockSpec(memory_space=pltpu.VMEM)


def moved(x, axis, by):
    peers = lax.axis_size(axis)
    return lax.ppermute(x, axis, [(i, i + by) for i in range(peers) if 0 <= i + by < peers])


def shift_row(value, row, target):
    cols = target.shape[2]
    wide = value.astype(F32)
    target[0, row] = value[:cols]
    for col_step in (1, 2):
        target[col_step, row] = wide[col_step : col_step + cols].astype(BF16)


def forward_kernel(joined_ref, weight_ref, out_weight_ref, hidden_ref, back_ref, even, odd, total,
                   back_total):
    step = pl.program_id(0)
    steps = pl.num_programs(0)
    _, rows, cols, width = even.shape
    tile = rows - 2

    def taps(now, before, shifting, multiply):
        def tap(t, carry):
            if multiply is not None:
                multiply(t, before)
            if shifting:
                for more in range(4):
                    row = jnp.minimum(4 * t + more, rows - 1)
                    shift_row(joined_ref[0, row], row, now)
            return carry

        lax.fori_loop(0, 9, tap, 0, unroll=True)

    def forward_tap(t, before):
        window = before[t % 3, pl.ds(t // 3, tile)].reshape(tile * cols, width)
        total[...] += jnp.dot(window, weight_ref[t], preferred_element_type=F32)

    def back_tap(t, before):
        window = before[2 - t % 3, pl.ds(2 - t // 3, tile)].reshape(tile * cols, width)
        back_total[...] += lax.dot_general(
            window, out_weight_ref[t], (((1,), (1,)), ((), ())), preferred_element_type=F32
        )

    @pl.when(step == 0)
    def _():
        total[...] = jnp.zeros_like(total)
        back_total[...] = jnp.zeros_like(back_total)
        taps(even, odd, True, None)

    @pl.when(step == 1)
    def _():
        taps(odd, even, True, back_tap)

    @pl.when((step > 1) & (step < steps - 1) & (step % 2 == 0))
    def _():
        taps(even, odd, True, forward_tap)

    @pl.when((step > 1) & (step < steps - 1) & (step % 2 == 1))
    def _():
        taps(odd, even, True, forward_tap)

    @pl.when(step == steps - 1)
    def _():
        taps(even, odd, False, forward_tap)
        pre = total[...]
        sigma = jax.nn.sigmoid(pre)
        hidden_ref[...] = (pre * sigma).astype(BF16)
        back = back_total[...] * (sigma * (1.0 + pre * (1.0 - sigma)))
        back_ref[...] = back.astype(BF16)


def forward(joined, cols, merge_weight, out_weight):
    layers, rows, _, width = joined.shape
    frames = layers - 1
    cells = (rows - 2) * cols
    return pl.pallas_call(
        forward_kernel,
        grid=(layers + 1,),
        in_specs=[
            pl.BlockSpec((1,) + joined.shape[1:], lambda i: (jnp.minimum(i, frames), 0, 0, 0)),
            pl.BlockSpec((9, width, width), lambda i: (0, jnp.maximum(i - 2, 0), 0)),
            pl.BlockSpec((9, width, width), lambda i: (0, 0, 0)),
        ],
        out_specs=[
            pl.BlockSpec((cells, width), lambda i: (0, 0)),
            pl.BlockSpec((cells, width), lambda i: (0, 0)),
        ],
        out_shape=[
            jax.ShapeDtypeStruct((cells, width), BF16),
            jax.ShapeDtypeStruct((cells, width), BF16),
        ],
        scratch_shapes=[
            pltpu.VMEM((3, rows, cols, width), BF16),
            pltpu.VMEM((3, rows, cols, width), BF16),
            pltpu.VMEM((cells, width), F32),
            pltpu.VMEM((cells, width), F32),
        ],
        compiler_params=PARAMS,
        cost_estimate=work(9 * cells * width * width * layers, 25_000_000),
        name="forward",
    )(joined, merge_weight, out_weight)


def layer_taps(own_row, other_row, own_right, other_right, out_ref, own_copies, other_copies, held):
    _, rows, cols, width = own_copies.shape
    tile, half = rows - 2, width // 2

    def product(copies, tap, right):
        window = copies[tap % 3, tap // 3 : tap // 3 + tile].reshape(tile * cols, width)
        return lax.dot_general(
            window, right[...], (((0,), (0,)), ((), ())), preferred_element_type=F32
        )

    for row in range(rows):
        shift_row(own_row(row), row, own_copies)
    for tap in range(9):
        held[tap] = product(own_copies, tap, own_right)
        for row in range(4 * tap, min(4 * tap + 4, rows)):
            shift_row(other_row(row), row, other_copies)
    for tap in range(9):
        value = held[tap] + product(other_copies, tap, other_right)
        for side in range(2):
            part = value[:, side * half : (side + 1) * half]
            out_ref[0, side, tap * width : (tap + 1) * width] = part.astype(BF16)


def layer_kernel(core_ref, own_ref, other_ref, own_right, other_right, *refs):
    layer_taps(
        lambda row: own_ref[0, row], lambda row: other_ref[0, row], own_right, other_right, *refs[-4:]
    )


def third_kernel(core_ref, own_ref, other_ref, own_hidden, other_hidden, own_back, other_back, own_cot,
                 other_cot, into_ref, out_ref, own_copies, other_copies, held, own_right, other_right):
    first = core_ref[0] == 0
    own_right[...] = jnp.where(first, own_back[...], own_cot[...])
    other_right[...] = jnp.where(first, other_back[...], other_cot[...])
    layer_taps(
        lambda row: jnp.where(first, own_ref[0, row], own_hidden[row]),
        lambda row: jnp.where(first, other_ref[0, row], other_hidden[row]),
        own_right,
        other_right,
        out_ref,
        own_copies,
        other_copies,
        held,
    )


def layer_gradient(place, core, cols, windows, hidden, rights, into=()):
    _, rows, wide_cols, width = windows[0].shape
    shape = (3, 2, 9 * width, width // 2)
    cells = (rows - 2) * cols
    if hidden:
        layer = pl.BlockSpec((1, rows, wide_cols, width), lambda i, at: (3, 0, 0, 0))
    else:
        layer = pl.BlockSpec(
            (1, rows, wide_cols, width), lambda i, at: (3 * at[0] + 1 + place, 0, 0, 0)
        )
    whole = pl.BlockSpec((rows, wide_cols, width), lambda i, at: (0, 0, 0))
    right = pl.BlockSpec((cells, width), lambda i, at: (0, 0))
    operands = (core, *windows, *hidden, *rights, *into)
    more = [pltpu.VMEM((cells, width), BF16)] * 2 if hidden else []
    return pl.pallas_call(
        third_kernel if hidden else layer_kernel,
        grid_spec=pltpu.PrefetchScalarGridSpec(
            num_scalar_prefetch=1,
            grid=(1,),
            in_specs=[layer] * 2
            + [whole] * len(hidden)
            + [right] * len(rights)
            + [pl.BlockSpec(memory_space=pl.ANY)] * len(into),
            out_specs=pl.BlockSpec((1,) + shape[1:], lambda i, at: (place, 0, 0, 0)),
            scratch_shapes=[
                pltpu.VMEM((3, rows, cols, width), BF16),
                pltpu.VMEM((3, rows, cols, width), BF16),
                pltpu.VMEM((9, width, width), F32),
            ]
            + more,
        ),
        out_shape=jax.ShapeDtypeStruct(shape, BF16),
        input_output_aliases={len(operands) - 1: 0} if into else {},
        compiler_params=PARAMS,
        cost_estimate=work(18 * cells * width * width, 5_000_000),
        name="layer_gradient",
    )(*operands)


def merged_kernel(hidden_ref, current_ref, weight_ref, merged_ref, copies, total):
    _, rows, cols, width = copies.shape
    tile = rows - 2
    for row in range(rows):
        shift_row(hidden_ref[row], row, copies)
    total[...] = current_ref[...].reshape(tile * cols, width).astype(F32)
    for tap in range(9):
        window = copies[tap % 3, tap // 3 : tap // 3 + tile].reshape(tile * cols, width)
        total[...] += jnp.dot(window, weight_ref[tap], preferred_element_type=F32)
    merged_ref[...] = total[...].astype(BF16).reshape(merged_ref.shape)


def merged_step(hidden_pad, current, out_weight):
    tile, cols, width = current.shape
    whole = [pl.BlockSpec(x.shape, lambda i: (0, 0, 0)) for x in (hidden_pad, current, out_weight)]
    return pl.pallas_call(
        merged_kernel,
        grid=(1,),
        in_specs=whole,
        out_specs=whole[1],
        out_shape=jax.ShapeDtypeStruct(current.shape, BF16),
        scratch_shapes=[
            pltpu.VMEM((3, tile + 2, cols, width), BF16),
            pltpu.VMEM((tile * cols, width), F32),
        ],
        compiler_params=PARAMS,
        cost_estimate=work(9 * tile * cols * width * width, 4_000_000),
        name="merged_step",
    )(hidden_pad, current, out_weight)


def final_kernel(base_ref, sums_ref, *refs):
    out_ref = refs[-1]
    taps, width, _ = out_ref.shape
    half = sums_ref.shape[-1]

    @pl.when(base_ref[0] + pl.program_id(0) < 5)
    def _():
        for side in range(2):
            part = sums_ref[0, side].reshape(taps, width, half)
            out_ref[:, :, side * half : (side + 1) * half] = part.astype(F32)


def final(base, sums, into=()):
    width = 2 * sums.shape[-1]
    return pl.pallas_call(
        final_kernel,
        grid_spec=pltpu.PrefetchScalarGridSpec(
            num_scalar_prefetch=1,
            grid=(3,),
            in_specs=[pl.BlockSpec((1,) + sums.shape[1:], lambda i, at: (i, 0, 0, 0))]
            + [pl.BlockSpec(memory_space=pl.ANY)] * len(into),
            out_specs=pl.BlockSpec(
                (9, width, width), lambda i, at: (0, jnp.minimum(at[0] + i, 4), 0)
            ),
        ),
        out_shape=jax.ShapeDtypeStruct((9, 5 * width, width), F32),
        input_output_aliases={2: 0} if into else {},
        compiler_params=PARAMS,
        cost_estimate=work(0, 12_000_000),
        name="final",
    )(base, sums, *into)


def shards(current, history, validity, offsets, merge_weight, out_weight, cotangent):
    tile, cols, width = current.shape
    frames = history.shape[0]
    ext = tile + 2
    core = lax.axis_index("core").astype(jnp.int32).reshape(1)
    valid = validity.astype(BF16)[..., None]
    masked12 = history[1:3] * valid[1:3]
    masked12, valid = lax.optimization_barrier((masked12, valid))
    masked = [history[0] * valid[0], masked12[0], masked12[1], history[3] * valid[3]]

    row_last = lax.axis_index(ROW) == lax.axis_size(ROW) - 1
    col_last = lax.axis_index(COL) == lax.axis_size(COL) - 1
    row_inside = (jnp.arange(ext) < ext - 1) | ~row_last
    ext_cols = cols + 2
    col_inside = (jnp.arange(ext_cols) < ext_cols - 1) | ~col_last
    inside = (row_inside[:, None] & col_inside[None, :]).astype(BF16)[..., None]

    left12 = moved(masked12, COL, 1)
    packed = moved(
        jnp.concatenate([masked[3][1:], masked[0][-3:], current[-1:], cotangent[-1:]], axis=0), ROW, 1
    )
    below = moved(jnp.concatenate([current[:1], cotangent[:1]], axis=0), ROW, -1)
    above3, above0 = packed[: tile - 1], packed[tile - 1 : tile + 2]
    near3 = jnp.concatenate([above3, masked[3][:3]], axis=0)
    near0 = jnp.concatenate([above0, masked[0][: tile - 1]], axis=0)
    now = jnp.concatenate([packed[tile + 2 : tile + 3], current, below[:1]], axis=0)
    cot = jnp.concatenate([packed[tile + 3 :], cotangent, below[1:]], axis=0)
    side = moved(
        jnp.concatenate([near3, near0[:, -3:], now[:, -1:], cot[:, -1:]], axis=1), COL, 1
    )
    right = moved(jnp.concatenate([now[:, :1], cot[:, :1]], axis=1), COL, -1)

    left12, right = lax.optimization_barrier((left12, right))

    def cols_of(k):
        wide = jnp.concatenate([left12[k - 1], masked[k]], axis=1)
        start = cols - 1 - offsets[k, 1]
        return lax.dynamic_slice(wide, (jnp.int32(0), start, jnp.int32(0)), (tile, ext_cols, width))

    wide1, wide2 = cols_of(1), cols_of(2)
    above12 = moved(jnp.concatenate([wide1[1:], wide2[1:]], axis=0), ROW, 1)

    def rows_of(above, wide, k):
        both = jnp.concatenate([above, wide], axis=0)
        start = tile - 2 - offsets[k, 0]
        return lax.dynamic_slice(both, (start, jnp.int32(0), jnp.int32(0)), (ext, ext_cols, width)) * inside

    blank = jnp.zeros((ext, -ext_cols % 8, width), BF16)

    def filled(*pieces):
        return jnp.concatenate([*pieces, blank], axis=1)

    joined = jnp.stack(
        [
            filled(side[:, cols + 4 :], cot, right[:, 1:]),
            filled(side[:, cols + 3 : cols + 4], now, right[:, :1]),
            filled(jnp.concatenate([side[:, cols : cols + 3], near0[:, : cols - 1]], axis=1) * inside),
            filled(rows_of(above12[: tile - 1], wide1, 1)),
            filled(rows_of(above12[tile - 1 :], wide2, 2)),
            filled(jnp.concatenate([side[:, 1:cols], near3[:, :3]], axis=1) * inside),
        ]
    )
    hidden, back_pre = forward(
        joined, cols, merge_weight.reshape(9, -1, width), out_weight.reshape(9, width, width)
    )
    first = core[0] == 0

    def swapped(x):
        return lax.ppermute(x, "core", SWAP)

    flat_cot = cotangent.reshape(tile * cols, width)
    windows = (joined, swapped(joined))

    hidden = hidden.reshape(tile, cols, width)
    hidden_above = moved(hidden[-1:], ROW, 1)
    hidden_below = moved(hidden[:1], ROW, -1)
    backs = (back_pre, swapped(back_pre))
    sums = layer_gradient(0, core, cols, windows, (), backs)
    sums, hidden_above, hidden_below, flat_cot = lax.optimization_barrier(
        (sums, hidden_above, hidden_below, flat_cot)
    )
    other_cot = swapped(flat_cot)
    hidden_pad = jnp.concatenate([hidden_above, hidden, hidden_below], axis=0)
    hidden_left = moved(hidden_pad[:, -1:], COL, 1)
    hidden_right = moved(hidden_pad[:, :1], COL, -1)
    sums = layer_gradient(1, core, cols, windows, (), backs, (sums,))
    sums, hidden_left, hidden_right, other_cot = lax.optimization_barrier(
        (sums, hidden_left, hidden_right, other_cot)
    )
    cots = (flat_cot, other_cot)
    hidden_pad = filled(hidden_left, hidden_pad, hidden_right)
    hiddens = (hidden_pad, swapped(hidden_pad))
    sums = layer_gradient(2, core, cols, windows, hiddens, (*backs, *cots), (sums,))
    merged = merged_step(hidden_pad, current, out_weight.reshape(9, width, width))

    chips = lax.axis_size(CHIPS)
    half = width // 2
    blocks = sums.reshape(chips, -1, half)
    got = lax.all_to_all(blocks, CHIPS, split_axis=0, concat_axis=0)
    got, merged = lax.optimization_barrier((got, merged))
    share = jnp.sum(got.astype(F32), axis=0).astype(BF16)
    spread = jnp.broadcast_to(share[None], blocks.shape)
    own = lax.all_to_all(spread, CHIPS, split_axis=0, concat_axis=0).reshape(sums.shape)
    other = swapped(own)
    merge_grad = final(3 * (1 - core), other, (final(3 * core, own),))
    merge_grad = merge_grad.reshape(merge_weight.shape)
    third = jnp.where(first, other[2], own[2])
    out_grad = jnp.concatenate([third[0], third[1]], axis=1).astype(F32).reshape(out_weight.shape)
    return (merged, merge_grad, out_grad)


def solution(mesh):
    parts = Mesh(mesh.devices.reshape(2, 2, 2, 4, 4), ("xh", "core", "xl", "z", "y"))
    return jax.shard_map(
        shards,
        mesh=parts,
        in_specs=(
            P(ROW, COL, None),
            P(None, ROW, COL, None),
            P(None, ROW, COL),
            P(),
            P(),
            P(),
            P(ROW, COL, None),
        ),
        out_specs=(P(ROW, COL, None), P(), P()),
        check_vma=False,
    )
```
